256 devices in a mesh: resp: 64 (over z_hi, x, y, core), tp: 4 (over z_lo).
Axes of the slice: x: 4, y: 4, z: 8 (z_hi: 2, z_lo: 4; z = z_hi * 4 + z_lo), core: 2. Of those that a mesh axis runs over, the one named last changes fastest.
Arguments:
- queries: bfloat16 [40960, 8192], P('resp', 'tp'), may hold values from -8 to 8
- resp_keys: bfloat16 [40960, 1024], P('resp', 'tp'), may hold values from -4 to 4
- resp_values: bfloat16 [40960, 1024], P('resp', 'tp'), may hold values from -4 to 4
- out_grad: bfloat16 [40960, 8192], P('resp', 'tp'), may hold values from -24 to 24
- prompt_keys: bfloat16 [4096, 1024], P(('resp', 'tp')), may hold values from -4 to 4
- prompt_values: bfloat16 [4096, 1024], P(('resp', 'tp')), may hold values from -4 to 4
- lengths: int32 [256], P('resp'), may hold values from 1 to 160, 25600 in all
- prompt_of: int32 [256], P('resp'), may hold values from 0 to 15, as said below
Outputs:
- attn_out: bfloat16 [40960, 8192], P('resp', 'tp')
- query_grad: bfloat16 [40960, 8192], P('resp', 'tp')
- resp_key_grad: bfloat16 [40960, 1024], P('resp', 'tp')
- resp_value_grad: bfloat16 [40960, 1024], P('resp', 'tp')
- prompt_key_grad: bfloat16 [4096, 1024], P(('resp', 'tp'))
- prompt_value_grad: bfloat16 [4096, 1024], P(('resp', 'tp'))
The draws below stay inside these ranges and needn't reach their ends.
Inputs may be any that keep to these rules, and one draw needn't show every extreme that they name: `prompt_of`: each prompt is named by exactly 16 responses.
All inputs are finite; a program needn't handle non-finite values. No bound on the sum of `lengths` on one device may be relied on, other than what follows from the above.
Results may differ from the reference program's by a relative error of at most 0.03.
Values may be sent and summed in bfloat16 or wider, within the bound.
No kernel may reach another device: no remote copies, remote signals or barrier semaphores. Data moves between devices by JAX's collectives and lax.ppermute only.
A program may use at most 128 MiB of HBM per device.

```python
import math
import jax
import jax.numpy as jnp
import numpy as np
from jax import lax

QHEADS = 64
KVHEADS = 8
HD = 128
GROUP = 16
LR = 160
LP = 256
RESPONSES = 256
PROMPTS = 16


def draw_queries(key, part):
    key = jax.random.fold_in(key, 11)
    return jnp.clip(jax.random.normal(key, (RESPONSES * LR, QHEADS * HD), jnp.float32), -4.0, 4.0).astype(jnp.bfloat16)


def draw_prompt_keys(key, part):
    key = jax.random.fold_in(key, 23)
    return jnp.clip(jax.random.normal(key, (PROMPTS * LP, KVHEADS * HD), jnp.float32), -4.0, 4.0).astype(jnp.bfloat16)


def draw_prompt_of(key, part):
    key = jax.random.fold_in(key, 37)
    return (jax.random.permutation(key, RESPONSES) // GROUP).astype(jnp.int32)


def block_levels(own_key, shape, cuts, least, high):
    factor_of, own = 1.0, jax.random.fold_in(own_key, 6)
    for axis_at, parts in cuts:
        steps = jnp.exp(jax.random.uniform(jax.random.fold_in(own, axis_at), (parts,), jnp.float32, least / len(cuts), high / len(cuts)))
        factor_of = factor_of * jnp.repeat(steps, shape[axis_at] // parts).reshape([-1 if axis == axis_at else 1 for axis in range(len(shape))])
    return factor_of


def split_up(number_of, total, most, skew):
    portions = [(1 << 20) // math.isqrt(grade ** skew) + 1 for grade in range(2, number_of + 1)]
    rest, holding = total - most - (number_of - 1), [1] * (number_of - 1)
    while rest > 0:
        candidates = [i for i in range(number_of - 1) if holding[i] < most]
        pool, remaining = sum([portions[i] for i in candidates]), rest
        for i in candidates:
            addition = min(most - holding[i], max(1, remaining * portions[i] // pool), rest)
            holding[i] = holding[i] + addition
            rest = rest - addition
    return np.array([most] + holding)


def ragged(stream_key, count, total, most, lean):
    if count == 2:
        one = jax.random.randint(stream_key, (), max(1, total - most), min(most, total - 1) + 1)
        return jnp.stack([one, total - one])
    sizes = jnp.asarray(split_up(count, total, most, lean), jnp.int32)
    pairs = (count - 1) // 2
    source_of, sink = sizes[1:1 + 2 * pairs:2], sizes[2:2 + 2 * pairs:2]
    room = jnp.minimum(source_of - 1, most - sink)
    passed = jax.random.randint(jax.random.fold_in(stream_key, 1), (pairs,), 0, 1 << 20) % (room + 1)
    sizes = sizes.at[1:1 + 2 * pairs:2].set(source_of - passed).at[2:2 + 2 * pairs:2].set(sink + passed)
    return sizes[jax.random.permutation(jax.random.fold_in(stream_key, 2), count)]


def normal_values(rng, extent, spread, bound, split=(), kind=jnp.bfloat16):
    array = jax.random.normal(rng, extent, jnp.float32) * spread
    if len(split) > 0:
        array = block_levels(rng, extent, split, -0.22, 0.18) * array
    return jnp.clip(array, min=-bound, max=bound).astype(kind)


def setup_inputs(seed: int = 0) -> dict:
    splits = jax.random.split(jax.random.key(seed), 9)
    queries = draw_queries(jax.random.fold_in(splits[8], 71), 0)
    resp_keys = normal_values(splits[1], (RESPONSES * LR, KVHEADS * HD), 1.0, 4.0, ((0, 64), (1, 4)))
    resp_values = normal_values(splits[2], (RESPONSES * LR, KVHEADS * HD), 1.0, 4.0, ((0, 64), (1, 4)))
    out_grad = normal_values(splits[3], (RESPONSES * LR, QHEADS * HD), 4.0, 24.0, ((0, 64), (1, 4)))
    prompt_keys = draw_prompt_keys(jax.random.fold_in(splits[8], 71), 0)
    prompt_values = normal_values(splits[5], (PROMPTS * LP, KVHEADS * HD), 1.0, 4.0, ((0, 256),))
    lengths = ragged(splits[6], RESPONSES, RESPONSES * LR * 5 // 8, LR, 1).astype(jnp.int32)
    prompt_of = draw_prompt_of(jax.random.fold_in(splits[8], 71), 0)
    return dict(queries=queries, resp_keys=resp_keys, resp_values=resp_values, out_grad=out_grad, prompt_keys=prompt_keys, prompt_values=prompt_values, lengths=lengths, prompt_of=prompt_of)


def lowered(values):
    return lax.optimization_barrier(values.astype(jnp.bfloat16)).astype(jnp.float32)


def respond(query_rows, key_rows, value_rows, grad_rows, prompt_key_rows, prompt_value_rows, length):
    query_count = query_rows.shape[0]
    prompt_count = prompt_key_rows.shape[0]
    kv_heads = key_rows.shape[1] // HD
    per_group = query_rows.shape[1] // (kv_heads * HD)
    score_scale = HD ** -0.5
    positions = jnp.arange(query_count)
    offsets = jnp.arange(prompt_count + query_count) - prompt_count
    valid_mask = positions < length
    allowed = (offsets[None, :] < 0) | ((offsets[None, :] <= positions[:, None]) & (offsets[None, :] < length))
    query_four = query_rows.astype(jnp.float32).reshape(query_count, kv_heads, per_group, HD)
    all_keys = jnp.concatenate([prompt_key_rows, key_rows], 0).astype(jnp.float32).reshape(-1, kv_heads, HD)
    all_values = jnp.concatenate([prompt_value_rows, value_rows], 0).astype(jnp.float32).reshape(-1, kv_heads, HD)
    grad_four = jnp.where(valid_mask[:, None], grad_rows.astype(jnp.float32), 0.0).reshape(query_count, kv_heads, per_group, HD)
    scores = jnp.einsum("qhgd,khd->hgqk", query_four, all_keys) * score_scale
    scores = jnp.where(allowed, scores, -1e30)
    largest = jnp.max(scores, axis=-1, keepdims=True)
    weights = jnp.where(allowed, jnp.exp(scores - largest), 0.0)
    probability = weights / jnp.sum(weights, axis=-1, keepdims=True) * valid_mask.astype(jnp.float32)[:, None]
    probability_low = lowered(probability)
    output = jnp.einsum("hgqk,khd->qhgd", probability_low, all_values).astype(jnp.bfloat16)
    output_wide = lax.optimization_barrier(output).astype(jnp.float32)
    delta_rows = jnp.sum(grad_four * output_wide, axis=-1)
    prob_grad = jnp.einsum("qhgd,khd->hgqk", grad_four, all_values)
    score_grad = lowered(probability * (prob_grad - jnp.transpose(delta_rows, (1, 2, 0))[..., None]))
    query_grad = (jnp.einsum("hgqk,khd->qhgd", score_grad, all_keys) * score_scale).astype(jnp.bfloat16)
    key_terms = jnp.einsum("hgqk,qhgd->khd", score_grad, query_four).reshape(-1, kv_heads * HD) * score_scale
    value_terms = jnp.einsum("hgqk,qhgd->khd", probability_low, grad_four).reshape(-1, kv_heads * HD)
    return (output.reshape(query_count, -1), query_grad.reshape(query_count, -1),
            key_terms[:prompt_count], value_terms[:prompt_count],
            key_terms[prompt_count:].astype(jnp.bfloat16), value_terms[prompt_count:].astype(jnp.bfloat16))


def reference(queries, resp_keys, resp_values, out_grad, prompt_keys, prompt_values, lengths, prompt_of):
    kv_width = KVHEADS * HD

    def visit(totals, number):
        key_sums, value_sums = totals
        first_row = number * LR
        owner_row = prompt_of[number] * LP
        results = respond(
            lax.dynamic_slice_in_dim(queries, first_row, LR, 0),
            lax.dynamic_slice_in_dim(resp_keys, first_row, LR, 0),
            lax.dynamic_slice_in_dim(resp_values, first_row, LR, 0),
            lax.dynamic_slice_in_dim(out_grad, first_row, LR, 0),
            lax.dynamic_slice_in_dim(prompt_keys, owner_row, LP, 0),
            lax.dynamic_slice_in_dim(prompt_values, owner_row, LP, 0),
            lengths[number])
        key_sums = lax.dynamic_update_slice_in_dim(
            key_sums, lax.dynamic_slice_in_dim(key_sums, owner_row, LP, 0) + results[2], owner_row, 0)
        value_sums = lax.dynamic_update_slice_in_dim(
            value_sums, lax.dynamic_slice_in_dim(value_sums, owner_row, LP, 0) + results[3], owner_row, 0)
        return (key_sums, value_sums), (results[0], results[1], results[4], results[5])

    blank_sums = jnp.zeros((PROMPTS * LP, kv_width), jnp.float32)
    (key_sums, value_sums), pieces = lax.scan(visit, (blank_sums, blank_sums), jnp.arange(RESPONSES, dtype=jnp.int32))
    attn_out = pieces[0].reshape(RESPONSES * LR, QHEADS * HD)
    query_grad = pieces[1].reshape(RESPONSES * LR, QHEADS * HD)
    resp_key_grad = pieces[2].reshape(RESPONSES * LR, kv_width)
    resp_value_grad = pieces[3].reshape(RESPONSES * LR, kv_width)
    return (attn_out, query_grad, resp_key_grad, resp_value_grad,
            key_sums.astype(jnp.bfloat16), value_sums.astype(jnp.bfloat16))
```

```python
import functools

import jax
import jax.numpy as jnp
from jax import lax
from jax.experimental import pallas as pl
from jax.experimental.pallas import tpu as pltpu
from jax.sharding import PartitionSpec as P

HD = 128
LP = 256
ROWS = 32
PER_GROUP = 8
KV_LANE = 2
LANES = 4
GROUPS = 4
TILE = 16
MEMBERS = 16
PROMPTS = 16
LOCAL = 4
SLICE = LP // GROUPS
HALF = LOCAL // 2
SENT = TILE + 8
LOG2E = 1.4426950408889634
SMALL = pltpu.CompilerParams(vmem_limit_bytes=16 * 1024 * 1024)

STORE_GROUPS = [
    [(p * 4 + (turn + t) % 4) * 4 + t for p in range(PROMPTS) for t in range(LANES)]
    for turn in range(4)
]
PICK_GROUPS = [
    [z * 32 + x * 8 + high * 4 + block for x in range(4) for block in range(4)]
    for z in range(2)
    for high in range(2)
]


def over_store(array):
    return lax.all_to_all(
        array,
        ("resp", "tp"),
        split_axis=0,
        concat_axis=0,
        tiled=True,
        axis_index_groups=STORE_GROUPS,
    )


def over_pick(array):
    return lax.all_to_all(
        array, "resp", split_axis=0, concat_axis=0, tiled=True, axis_index_groups=PICK_GROUPS
    )


def column_of(x):
    return (x // KV_LANE, x % KV_LANE)


def stored_kernel(owner_ref, key_ref, value_ref, out_ref):
    at = lax.broadcasted_iota(jnp.int32, (SENT - TILE, HD), 1)
    asked = jnp.zeros((SENT - TILE, HD), jnp.int32)
    for one in range(LOCAL):
        asked = jnp.where(at == one, owner_ref[one], asked)
    asked = asked.astype(jnp.float32).astype(jnp.bfloat16)
    for prompt in range(PROMPTS):
        which, head = column_of(prompt // 2 % 4)
        source = value_ref if which else key_ref
        for lane in range(LANES):
            first = (lane * KV_LANE + head) * HD
            out_ref[prompt * LANES + lane, :TILE] = source[:, first : first + HD]
            out_ref[prompt * LANES + lane, TILE:] = asked


def pick_kernel(pieces_ref, first_ref, second_ref, owner_ref, owners, sem):
    resp = lax.axis_index("resp")
    prompt = resp // 4
    turn = (resp % 4 + LANES - lax.axis_index("tp")) % 4
    for x in range(4):
        for block in range(4):
            source = (prompt // 8 * 8 + x * 2 + prompt % 2) * LANES + (block + 4 - turn) % 4
            tile = pieces_ref[source, TILE:].astype(jnp.float32)
            owner_ref[x * 4 + block : x * 4 + block + 1] = tile[:1].astype(jnp.int32)
    copy = pltpu.make_async_copy(owner_ref, owners, sem)
    copy.start()
    copy.wait()
    for member in range(MEMBERS):
        for one in range(LOCAL):
            owner = owners[member, one]
            out_ref = first_ref if one < HALF else second_ref
            for lane in range(LANES):
                out_ref[member, one % HALF, lane * TILE : (lane + 1) * TILE] = pieces_ref[
                    owner * LANES + lane, :TILE
                ]


def fold_kernel(owner_ref, first_ref, second_ref, out_ref, total):
    total[...] = jnp.zeros_like(total)
    for one in range(LOCAL):
        terms_ref = first_ref if one < HALF else second_ref
        for member in range(MEMBERS):
            owner = owner_ref[member, one]
            total[owner] += terms_ref[member, one % HALF].astype(jnp.float32)
    for prompt in range(PROMPTS):
        for lane in range(LANES):
            out_ref[prompt * LANES + lane] = total[
                prompt, lane * TILE : (lane + 1) * TILE
            ].astype(out_ref.dtype)


def summed_kernel(sums_ref, key_ref, value_ref):
    for x in range(4):
        which, head = column_of(x)
        target = value_ref if which else key_ref
        for lane in range(LANES):
            tile = jnp.zeros((TILE, HD), jnp.float32)
            for z in range(2):
                for high in range(2):
                    source = (z * 8 + x * 2 + high) * LANES + lane
                    tile = tile + sums_ref[source].astype(jnp.float32)
            first = (lane * KV_LANE + head) * HD
            target[:, first : first + HD] = tile.astype(target.dtype)


def attend_kernel(
    first_response, length_ref, query_ref, grad_ref, key_ref, value_ref, prompt_ref, *rest
):
    rest = rest[-17:]
    out_ref, query_grad_ref, key_grad_ref, value_grad_ref, prompt_grad_ref = rest[:5]
    keys, values, keys_t, values_t, stacked_query, stacked_grad = rest[5:11]
    scores, prob_grads, probability_low, score_grad, key_total, value_total = rest[11:]
    length = length_ref[first_response + pl.program_id(0)]
    span = query_ref.shape[0]
    scale = HD**-0.5
    wide = PER_GROUP * ROWS
    key_total[...] = jnp.zeros_like(key_total)
    value_total[...] = jnp.zeros_like(value_total)
    for head in range(KV_LANE):
        for whole, whole_t, own_ref, which in (
            (keys, keys_t, key_ref, 0),
            (values, values_t, value_ref, 1),
        ):
            whole[head, :LP] = prompt_ref[which, head, :, 0].reshape(LP, HD)
            whole[head, LP:] = own_ref[:, head * HD : (head + 1) * HD]
            whole_t[head] = whole[head].T

    def heads(slot, head):
        for at in range(PER_GROUP):
            column = (head * PER_GROUP + at) * HD
            yield slice(at * ROWS, (at + 1) * ROWS), slice(column, column + HD)

    def score(slot, head, first):
        count = LP + first + ROWS
        lane = lax.broadcasted_iota(jnp.int32, (1, wide), 1) % ROWS
        causal = lax.broadcasted_iota(jnp.int32, (ROWS, 1), 0) <= lane
        for part, column in heads(slot, head):
            stacked_query[slot, part] = query_ref[first : first + ROWS, column]
            stacked_grad[slot, part] = grad_ref[first : first + ROWS, column]
        raw = lax.dot_general(
            keys[head, :count],
            stacked_query[slot],
            (((1,), (1,)), ((), ())),
            preferred_element_type=jnp.float32,
        )
        tail = jnp.where(causal, raw[count - ROWS :], -1e30)
        scores[slot, : count - ROWS] = raw[: count - ROWS]
        scores[slot, count - ROWS : count] = tail
        top = jnp.max(raw[: count - ROWS].reshape(-1, 8, wide), axis=0)
        top = jnp.maximum(top, jnp.max(tail.reshape(-1, 8, wide), axis=0))
        prob_grads[slot, :count] = lax.dot_general(
            values[head, :count],
            stacked_grad[slot],
            (((1,), (1,)), ((), ())),
            preferred_element_type=jnp.float32,
        )
        return jnp.max(top, axis=0, keepdims=True) * (scale * LOG2E)

    def soften(slot, head, first, largest):
        count = LP + first + ROWS
        lane = lax.broadcasted_iota(jnp.int32, (1, wide), 1) % ROWS
        live = first + lane < length
        blocks = [slice(at, at + ROWS) for at in range(0, count, ROWS)]
        total = jnp.zeros((8, wide), jnp.float32)
        for block in blocks:
            weights = jnp.exp2(scores[slot, block] * (scale * LOG2E) - largest)
            scores[slot, block] = weights
            total = total + jnp.sum(weights.reshape(-1, 8, wide), axis=0)
        inverse = jnp.where(live, 1.0 / jnp.sum(total, axis=0, keepdims=True), 0.0)
        total = jnp.zeros((8, wide), jnp.float32)
        for block in blocks:
            probability = scores[slot, block] * inverse
            probability_low[slot, block] = probability.astype(jnp.bfloat16)
            terms = probability * prob_grads[slot, block]
            total = total + jnp.sum(terms.reshape(-1, 8, wide), axis=0)
        delta = jnp.sum(total, axis=0, keepdims=True)
        for block in blocks:
            probability = scores[slot, block] * inverse
            score_grad[slot, block] = (probability * (prob_grads[slot, block] - delta)).astype(
                jnp.bfloat16
            )

    def spread(slot, head, first):
        count = LP + first + ROWS
        rows = slice(first, first + ROWS)
        output = (
            jnp.dot(
                values_t[head, :, :count],
                probability_low[slot, :count],
                preferred_element_type=jnp.float32,
            )
            .astype(jnp.bfloat16)
            .T
        )
        query_grad = (
            (
                jnp.dot(
                    keys_t[head, :, :count],
                    score_grad[slot, :count],
                    preferred_element_type=jnp.float32,
                )
                * scale
            )
            .astype(jnp.bfloat16)
            .T
        )
        for part, column in heads(slot, head):
            out_ref[rows, column] = output[part]
            query_grad_ref[rows, column] = query_grad[part]
        value_total[head, :count] += jnp.dot(
            probability_low[slot, :count], stacked_grad[slot], preferred_element_type=jnp.float32
        )
        key_total[head, :count] += jnp.dot(
            score_grad[slot, :count], stacked_query[slot], preferred_element_type=jnp.float32
        )

    def work(firsts):
        streams = [(head, first) for first in firsts for head in range(KV_LANE)]
        largest = {0: score(0, *streams[0])}
        for slot, stream in enumerate(streams):
            if slot + 1 < len(streams):
                largest[slot + 1] = score(slot + 1, *streams[slot + 1])
            soften(slot, *stream, largest[slot])
            spread(slot, *stream)

    def blank(first, last):
        zeros = jnp.zeros((last - first, query_ref.shape[1]), jnp.bfloat16)
        out_ref[first:last, :] = zeros
        query_grad_ref[first:last, :] = zeros

    for first in range(0, span, 2 * ROWS):
        second = first + ROWS
        last = min(second + ROWS, span)
        if second < span:

            @pl.when(length > second)
            def _():
                work((first, second))

        @pl.when((length > first) & ((length <= second) | (second >= span)))
        def _():
            work((first,))
            if second < span:
                blank(second, last)

        @pl.when(length <= first)
        def _():
            blank(first, last)

    for head in range(KV_LANE):
        lanes = slice(head * HD, (head + 1) * HD)
        key_terms = (key_total[head] * scale).astype(jnp.bfloat16)
        value_terms = value_total[head].astype(jnp.bfloat16)
        prompt_grad_ref[0, head, :, 0] = key_terms[:LP].reshape(GROUPS, SLICE, HD)
        prompt_grad_ref[1, head, :, 0] = value_terms[:LP].reshape(GROUPS, SLICE, HD)
        key_grad_ref[:, lanes] = key_terms[LP:]
        value_grad_ref[:, lanes] = value_terms[LP:]


def attend(
    lengths, queries, out_grad, resp_keys, resp_values, prompt_rows, first=0, earlier=()
):
    count = prompt_rows.shape[3]
    span = queries.shape[0] // lengths.shape[0]
    wide = pl.BlockSpec((span, queries.shape[1]), lambda i, length: (first + i, 0))
    narrow = pl.BlockSpec((span, resp_keys.shape[1]), lambda i, length: (first + i, 0))
    prompt = pl.BlockSpec(
        (2, KV_LANE, GROUPS, 1, SLICE, HD), lambda i, length: (0, 0, 0, i, 0, 0)
    )
    both = LP + span
    streams = 2 * KV_LANE
    stacked = PER_GROUP * ROWS
    return pl.pallas_call(
        functools.partial(attend_kernel, first),
        out_shape=(
            jax.ShapeDtypeStruct(queries.shape, jnp.bfloat16),
            jax.ShapeDtypeStruct(queries.shape, jnp.bfloat16),
            jax.ShapeDtypeStruct(resp_keys.shape, jnp.bfloat16),
            jax.ShapeDtypeStruct(resp_keys.shape, jnp.bfloat16),
            jax.ShapeDtypeStruct(prompt_rows.shape, jnp.bfloat16),
        ),
        grid_spec=pltpu.PrefetchScalarGridSpec(
            num_scalar_prefetch=1,
            grid=(count,),
            in_specs=[wide, wide, narrow, narrow, prompt]
            + [pl.BlockSpec(memory_space=pl.ANY)] * len(earlier),
            out_specs=[wide, wide, narrow, narrow, prompt],
            scratch_shapes=[
                pltpu.VMEM((KV_LANE, both, HD), jnp.bfloat16),
                pltpu.VMEM((KV_LANE, both, HD), jnp.bfloat16),
                pltpu.VMEM((KV_LANE, HD, both), jnp.bfloat16),
                pltpu.VMEM((KV_LANE, HD, both), jnp.bfloat16),
                pltpu.VMEM((streams, stacked, HD), jnp.bfloat16),
                pltpu.VMEM((streams, stacked, HD), jnp.bfloat16),
                pltpu.VMEM((streams, both, stacked), jnp.float32),
                pltpu.VMEM((streams, both, stacked), jnp.float32),
                pltpu.VMEM((streams, both, stacked), jnp.bfloat16),
                pltpu.VMEM((streams, both, stacked), jnp.bfloat16),
                pltpu.VMEM((KV_LANE, both, HD), jnp.float32),
                pltpu.VMEM((KV_LANE, both, HD), jnp.float32),
            ],
        ),
        input_output_aliases={6 + at: at for at in range(len(earlier))},
        compiler_params=pltpu.CompilerParams(vmem_limit_bytes=32 * 1024 * 1024),
        cost_estimate=pl.CostEstimate(
            flops=24 * count * span * queries.shape[1] * both,
            bytes_accessed=8 * count * span * queries.shape[1],
            transcendentals=count * span * queries.shape[1] * both // HD,
        ),
    )(lengths, queries, out_grad, resp_keys, resp_values, prompt_rows, *earlier)


def in_vmem(kernel, out_shape, *operands, scalars=0, **more):
    spaces = [pltpu.SMEM] * scalars + [pltpu.VMEM] * (len(operands) - scalars)
    return pl.pallas_call(
        kernel,
        out_shape=out_shape,
        in_specs=[pl.BlockSpec(memory_space=space) for space in spaces],
        compiler_params=SMALL,
        **more,
    )(*operands)


def low(*shape):
    return jax.ShapeDtypeStruct(shape, jnp.bfloat16)


def shards(
    queries, resp_keys, resp_values, out_grad, prompt_keys, prompt_values, lengths, prompt_of
):
    pieces = over_store(
        in_vmem(
            stored_kernel,
            low(PROMPTS * LANES, SENT, HD),
            prompt_of,
            prompt_keys,
            prompt_values,
            scalars=1,
        )
    )
    *picked, owners = in_vmem(
        pick_kernel,
        (low(MEMBERS, HALF, SLICE, HD),) * 2
        + (jax.ShapeDtypeStruct((MEMBERS, HD), jnp.int32),),
        pieces,
        scratch_shapes=[pltpu.SMEM((MEMBERS, HD), jnp.int32), pltpu.SemaphoreType.DMA],
    )
    picked = [over_pick(part) for part in picked]
    results, terms = (), []
    for half in range(2):
        *results, part = attend(
            lengths,
            queries,
            out_grad,
            resp_keys,
            resp_values,
            picked[half].reshape(2, KV_LANE, GROUPS, HALF, SLICE, HD),
            half * HALF,
            results,
        )
        terms.append(over_pick(part.reshape(MEMBERS, HALF, SLICE, HD)))
    sums = in_vmem(
        fold_kernel,
        low(PROMPTS * LANES, TILE, HD),
        owners,
        *terms,
        scalars=1,
        scratch_shapes=[pltpu.VMEM((PROMPTS, SLICE, HD), jnp.float32)],
    )
    prompt_key_grad, prompt_value_grad = in_vmem(
        summed_kernel,
        (low(*prompt_keys.shape), low(*prompt_values.shape)),
        over_store(sums),
    )
    return (*results, prompt_key_grad, prompt_value_grad)


def solution(mesh):
    wide = P("resp", "tp")
    stored = P(("resp", "tp"), None)
    return jax.shard_map(
        shards,
        mesh=mesh,
        in_specs=(wide, wide, wide, wide, stored, stored, P("resp"), P("resp")),
        out_specs=(wide, wide, wide, wide, stored, stored),
        check_vma=False,
    )
```

```python
import jax
import jax.numpy as jnp
from jax import lax
from jax.experimental import pallas as pl
from jax.experimental.pallas import tpu as pltpu
from jax.sharding import PartitionSpec as P

HD = 128
LP = 256
ROWS = 32
PER_GROUP = 8
KV_LANE = 2
LANES = 4
GROUPS = 4
TILE = 16
MEMBERS = 16
PROMPTS = 16
LOCAL = 4
SLICE = LP // GROUPS
CHUNKS = 5
SENT = TILE + 8
LOG2E = 1.4426950408889634
LARGE = pltpu.CompilerParams(vmem_limit_bytes=48 * 1024 * 1024)
SMALL = pltpu.CompilerParams(vmem_limit_bytes=16 * 1024 * 1024)

STORE_GROUPS = [
    [(p * 4 + (turn + t) % 4) * 4 + t for p in range(PROMPTS) for t in range(LANES)]
    for turn in range(4)
]
PICK_GROUPS = [
    [z * 32 + x * 8 + high * 4 + block for x in range(4) for block in range(4)]
    for z in range(2)
    for high in range(2)
]


def over_store(array):
    return lax.all_to_all(
        array,
        ("resp", "tp"),
        split_axis=0,
        concat_axis=0,
        tiled=True,
        axis_index_groups=STORE_GROUPS,
    )


def over_pick(array):
    return lax.all_to_all(
        array, "resp", split_axis=0, concat_axis=0, tiled=True, axis_index_groups=PICK_GROUPS
    )


def column_of(x):
    return (x // KV_LANE, x % KV_LANE)


def stored_kernel(
    owner_hbm, key_hbm, value_hbm, out_ref, owner_ref, key_ref, value_ref, sems
):
    copies = [
        pltpu.make_async_copy(source, target, sems.at[at])
        for at, (source, target) in enumerate(
            ((owner_hbm, owner_ref), (key_hbm, key_ref), (value_hbm, value_ref))
        )
    ]
    for copy in copies:
        copy.start()
    for copy in copies:
        copy.wait()
    at = lax.broadcasted_iota(jnp.int32, (SENT - TILE, HD), 1)
    asked = jnp.zeros((SENT - TILE, HD), jnp.int32)
    for one in range(LOCAL):
        asked = jnp.where(at == one, owner_ref[one], asked)
    asked = asked.astype(jnp.float32).astype(jnp.bfloat16)
    for prompt in range(PROMPTS):
        which, head = column_of(prompt // 2 % 4)
        source = value_ref if which else key_ref
        for lane in range(LANES):
            first = (lane * KV_LANE + head) * HD
            out_ref[prompt * LANES + lane] = jnp.concatenate(
                [source[:, first : first + HD], asked], 0
            )


def pick_kernel(pieces_ref, out_ref, owner_ref, owners, sem):
    resp = lax.axis_index("resp")
    prompt = resp // 4
    turn = (resp % 4 + LANES - lax.axis_index("tp")) % 4
    for x in range(4):
        for block in range(4):
            source = (prompt // 8 * 8 + x * 2 + prompt % 2) * LANES + (block + 4 - turn) % 4
            tile = pieces_ref[source].astype(jnp.float32)
            owner_ref[x * 4 + block : x * 4 + block + 1] = tile[TILE : TILE + 1].astype(jnp.int32)
    copy = pltpu.make_async_copy(owner_ref, owners, sem)
    copy.start()
    copy.wait()
    for member in range(MEMBERS):
        for one in range(LOCAL):
            owner = owners[member, one]
            for lane in range(LANES):
                out_ref[member, one, lane * TILE : (lane + 1) * TILE] = pieces_ref[
                    owner * LANES + lane, :TILE
                ]


def fold_kernel(owner_ref, terms_ref, token_ref, out_ref, total):
    total[...] = jnp.zeros_like(total)
    for one in range(LOCAL):
        for member in range(MEMBERS):
            owner = owner_ref[member, one]
            total[owner] += terms_ref[member, one].astype(jnp.float32)
    for prompt in range(PROMPTS):
        for lane in range(LANES):
            out_ref[prompt * LANES + lane] = total[
                prompt, lane * TILE : (lane + 1) * TILE
            ].astype(out_ref.dtype)


def summed_kernel(sums_ref, key_ref, value_ref):
    for x in range(4):
        which, head = column_of(x)
        target = value_ref if which else key_ref
        for lane in range(LANES):
            tile = jnp.zeros((TILE, HD), jnp.float32)
            for z in range(2):
                for high in range(2):
                    source = (z * 8 + x * 2 + high) * LANES + lane
                    tile = tile + sums_ref[source].astype(jnp.float32)
            first = (lane * KV_LANE + head) * HD
            target[:, first : first + HD] = tile.astype(target.dtype)


def heads(head):
    for at in range(PER_GROUP):
        column = (head * PER_GROUP + at) * HD
        yield slice(at * ROWS, (at + 1) * ROWS), slice(column, column + HD)


def by_length(length, span, work, blank):
    for first in range(0, span, 2 * ROWS):
        second = first + ROWS
        last = min(second + ROWS, span)
        if second < span:

            @pl.when(length > second)
            def _():
                work((first, second))

        @pl.when((length > first) & ((length <= second) | (second >= span)))
        def _():
            work((first,))
            if second < span:
                blank(second, last)

        @pl.when(length <= first)
        def _():
            blank(first, last)


def attend_kernel(
    length_ref,
    query_ref,
    grad_ref,
    key_ref,
    value_ref,
    prompt_ref,
    key_grad_ref,
    value_grad_ref,
    prompt_grad_ref,
    probability_ref,
    score_grad_ref,
    keys,
    values,
    stacked_query,
    stacked_grad,
    scores,
    prob_grads,
    key_total,
    value_total,
):
    length = length_ref[pl.program_id(0)]
    span = query_ref.shape[0]
    scale = HD**-0.5
    wide = PER_GROUP * ROWS
    for head in range(KV_LANE):
        for whole, own_ref, which in ((keys, key_ref, 0), (values, value_ref, 1)):
            whole[head, :LP] = prompt_ref[which, head, :, 0].reshape(LP, HD)
            whole[head, LP:] = own_ref[:, head * HD : (head + 1) * HD]

    def score(slot, head, first):
        count = LP + first + ROWS
        lane = lax.broadcasted_iota(jnp.int32, (1, wide), 1) % ROWS
        causal = lax.broadcasted_iota(jnp.int32, (ROWS, 1), 0) <= lane
        for part, column in heads(head):
            stacked_query[slot, part] = query_ref[first : first + ROWS, column]
            stacked_grad[slot, part] = grad_ref[first : first + ROWS, column]
        raw = lax.dot_general(
            keys[head, :count],
            stacked_query[slot],
            (((1,), (1,)), ((), ())),
            preferred_element_type=jnp.float32,
        )
        tail = jnp.where(causal, raw[count - ROWS :], -1e30)
        scores[slot, : count - ROWS] = raw[: count - ROWS]
        scores[slot, count - ROWS : count] = tail
        top = jnp.max(raw[: count - ROWS].reshape(-1, 8, wide), axis=0)
        top = jnp.maximum(top, jnp.max(tail.reshape(-1, 8, wide), axis=0))
        prob_grads[slot, :count] = lax.dot_general(
            values[head, :count],
            stacked_grad[slot],
            (((1,), (1,)), ((), ())),
            preferred_element_type=jnp.float32,
        )
        return jnp.max(top, axis=0, keepdims=True) * (scale * LOG2E)

    def soften(slot, head, first, largest):
        count = LP + first + ROWS
        chunk = first // ROWS
        lane = lax.broadcasted_iota(jnp.int32, (1, wide), 1) % ROWS
        live = first + lane < length
        blocks = [slice(at, at + ROWS) for at in range(0, count, ROWS)]
        total = jnp.zeros((8, wide), jnp.float32)
        for block in blocks:
            weights = jnp.exp2(scores[slot, block] * (scale * LOG2E) - largest)
            scores[slot, block] = weights
            total = total + jnp.sum(weights.reshape(-1, 8, wide), axis=0)
        inverse = jnp.where(live, 1.0 / jnp.sum(total, axis=0, keepdims=True), 0.0)
        total = jnp.zeros((8, wide), jnp.float32)
        for block in blocks:
            probability = scores[slot, block] * inverse
            probability_ref[0, head, chunk, block] = probability.astype(jnp.bfloat16)
            terms = probability * prob_grads[slot, block]
            total = total + jnp.sum(terms.reshape(-1, 8, wide), axis=0)
        delta = jnp.sum(total, axis=0, keepdims=True)
        for block in blocks:
            probability = scores[slot, block] * inverse
            score_grad_ref[0, head, chunk, block] = (
                probability * (prob_grads[slot, block] - delta)
            ).astype(jnp.bfloat16)

    def gather(slot, head, first):
        count = LP + first + ROWS
        chunk = first // ROWS
        for total, left_ref, stacked in (
            (value_total, probability_ref, stacked_grad),
            (key_total, score_grad_ref, stacked_query),
        ):
            terms = jnp.dot(
                left_ref[0, head, chunk, :count],
                stacked[slot],
                preferred_element_type=jnp.float32,
            )
            if first == 0:
                total[head, :count] = terms
            else:
                total[head, : count - ROWS] += terms[: count - ROWS]
                total[head, count - ROWS : count] = terms[count - ROWS :]

    def work(firsts):
        streams = [(head, first) for first in firsts for head in range(KV_LANE)]
        largest = {0: score(0, *streams[0])}
        for slot, stream in enumerate(streams):
            if slot + 1 < len(streams):
                largest[slot + 1] = score(slot + 1, *streams[slot + 1])
            soften(slot, *stream, largest[slot])
            gather(slot, *stream)

    def blank(first, last):
        zeros = jnp.zeros((KV_LANE, last - first, HD), jnp.float32)
        key_total[:, LP + first : LP + last] = zeros
        value_total[:, LP + first : LP + last] = zeros

    by_length(length, span, work, blank)

    for head in range(KV_LANE):
        lanes = slice(head * HD, (head + 1) * HD)
        key_terms = (key_total[head] * scale).astype(jnp.bfloat16)
        value_terms = value_total[head].astype(jnp.bfloat16)
        prompt_grad_ref[0, head, :, 0] = key_terms[:LP].reshape(GROUPS, SLICE, HD)
        prompt_grad_ref[1, head, :, 0] = value_terms[:LP].reshape(GROUPS, SLICE, HD)
        key_grad_ref[:, lanes] = key_terms[LP:]
        value_grad_ref[:, lanes] = value_terms[LP:]


def outputs_kernel(
    length_ref,
    key_ref,
    value_ref,
    prompt_ref,
    probability_ref,
    score_grad_ref,
    out_ref,
    query_grad_ref,
    token_ref,
    keys_t,
    values_t,
):
    length = length_ref[pl.program_id(0)]
    span = out_ref.shape[0]
    scale = HD**-0.5
    for head in range(KV_LANE):
        lanes = slice(head * HD, (head + 1) * HD)
        for whole_t, own_ref, which in ((keys_t, key_ref, 0), (values_t, value_ref, 1)):
            whole_t[head] = jnp.concatenate(
                [prompt_ref[which, head, :, 0].reshape(LP, HD), own_ref[:, lanes]], 0
            ).T

    def work(firsts):
        for first in firsts:
            count = LP + first + ROWS
            chunk = first // ROWS
            rows = slice(first, first + ROWS)
            for head in range(KV_LANE):
                output = jnp.dot(
                    values_t[head, :, :count],
                    probability_ref[0, head, chunk, :count],
                    preferred_element_type=jnp.float32,
                )
                query_grad = jnp.dot(
                    keys_t[head, :, :count],
                    score_grad_ref[0, head, chunk, :count],
                    preferred_element_type=jnp.float32,
                )
                output = output.astype(jnp.bfloat16).T
                query_grad = (query_grad * scale).astype(jnp.bfloat16).T
                for part, column in heads(head):
                    out_ref[rows, column] = output[part]
                    query_grad_ref[rows, column] = query_grad[part]

    def blank(first, last):
        zeros = jnp.zeros((last - first, out_ref.shape[1]), jnp.bfloat16)
        out_ref[first:last, :] = zeros
        query_grad_ref[first:last, :] = zeros

    by_length(length, span, work, blank)
    token_ref[...] = jnp.zeros_like(token_ref)


def specs(span, wide, narrow):
    both = LP + span
    stacked = PER_GROUP * ROWS
    return dict(
        wide=pl.BlockSpec((span, wide), lambda i, length: (i, 0)),
        narrow=pl.BlockSpec((span, narrow), lambda i, length: (i, 0)),
        prompt=pl.BlockSpec(
            (2, KV_LANE, GROUPS, 1, SLICE, HD), lambda i, length: (0, 0, 0, i, 0, 0)
        ),
        kept=pl.BlockSpec(
            (1, KV_LANE, CHUNKS, both, stacked), lambda i, length: (i, 0, 0, 0, 0)
        ),
    )


def attend(lengths, queries, out_grad, resp_keys, resp_values, prompt_rows):
    count = lengths.shape[0]
    span = queries.shape[0] // count
    both = LP + span
    streams = 2 * KV_LANE
    stacked = PER_GROUP * ROWS
    spec = specs(span, queries.shape[1], resp_keys.shape[1])
    kept = jax.ShapeDtypeStruct((count, KV_LANE, CHUNKS, both, stacked), jnp.bfloat16)
    return pl.pallas_call(
        attend_kernel,
        out_shape=(
            jax.ShapeDtypeStruct(resp_keys.shape, jnp.bfloat16),
            jax.ShapeDtypeStruct(resp_keys.shape, jnp.bfloat16),
            jax.ShapeDtypeStruct(prompt_rows.shape, jnp.bfloat16),
            kept,
            kept,
        ),
        grid_spec=pltpu.PrefetchScalarGridSpec(
            num_scalar_prefetch=1,
            grid=(count,),
            in_specs=[spec[name] for name in ("wide", "wide", "narrow", "narrow", "prompt")],
            out_specs=[spec[name] for name in ("narrow", "narrow", "prompt", "kept", "kept")],
            scratch_shapes=[
                pltpu.VMEM((KV_LANE, both, HD), jnp.bfloat16),
                pltpu.VMEM((KV_LANE, both, HD), jnp.bfloat16),
                pltpu.VMEM((streams, stacked, HD), jnp.bfloat16),
                pltpu.VMEM((streams, stacked, HD), jnp.bfloat16),
                pltpu.VMEM((streams, both, stacked), jnp.float32),
                pltpu.VMEM((streams, both, stacked), jnp.float32),
                pltpu.VMEM((KV_LANE, both, HD), jnp.float32),
                pltpu.VMEM((KV_LANE, both, HD), jnp.float32),
            ],
        ),
        compiler_params=LARGE,
        cost_estimate=pl.CostEstimate(
            flops=16 * queries.size * both,
            bytes_accessed=4 * queries.size,
            transcendentals=queries.size * both // HD,
        ),
    )(lengths, queries, out_grad, resp_keys, resp_values, prompt_rows)


def outputs(lengths, resp_keys, resp_values, prompt_rows, probability, score_grad, wide):
    count = lengths.shape[0]
    rows = resp_keys.shape[0]
    span = rows // count
    both = LP + span
    spec = specs(span, wide, resp_keys.shape[1])
    shape = jax.ShapeDtypeStruct((rows, wide), jnp.bfloat16)
    return pl.pallas_call(
        outputs_kernel,
        out_shape=(shape, shape, jax.ShapeDtypeStruct((8, HD), jnp.int32)),
        grid_spec=pltpu.PrefetchScalarGridSpec(
            num_scalar_prefetch=1,
            grid=(count,),
            in_specs=[spec[name] for name in ("narrow", "narrow", "prompt", "kept", "kept")],
            out_specs=[
                spec["wide"],
                spec["wide"],
                pl.BlockSpec((8, HD), lambda i, length: (0, 0)),
            ],
            scratch_shapes=[
                pltpu.VMEM((KV_LANE, HD, both), jnp.bfloat16),
                pltpu.VMEM((KV_LANE, HD, both), jnp.bfloat16),
            ],
        ),
        compiler_params=LARGE,
        cost_estimate=pl.CostEstimate(
            flops=8 * rows * wide * both,
            bytes_accessed=4 * rows * wide + 4 * probability.size,
            transcendentals=0,
        ),
    )(lengths, resp_keys, resp_values, prompt_rows, probability, score_grad)


def whole(kernel, out_shape, spaces, *operands, **more):
    return pl.pallas_call(
        kernel,
        out_shape=out_shape,
        in_specs=[pl.BlockSpec(memory_space=space) for space in spaces],
        compiler_params=SMALL,
        **more,
    )(*operands)


def low(*shape):
    return jax.ShapeDtypeStruct(shape, jnp.bfloat16)


def shards(
    queries, resp_keys, resp_values, out_grad, prompt_keys, prompt_values, lengths, prompt_of
):
    pieces = over_store(
        whole(
            stored_kernel,
            low(PROMPTS * LANES, SENT, HD),
            [pltpu.HBM] * 3,
            prompt_of,
            prompt_keys,
            prompt_values,
            scratch_shapes=[
                pltpu.SMEM(prompt_of.shape, jnp.int32),
                pltpu.VMEM(prompt_keys.shape, jnp.bfloat16),
                pltpu.VMEM(prompt_values.shape, jnp.bfloat16),
                pltpu.SemaphoreType.DMA((3,)),
            ],
        )
    )
    picked, owners = whole(
        pick_kernel,
        (low(MEMBERS, LOCAL, SLICE, HD), jax.ShapeDtypeStruct((MEMBERS, HD), jnp.int32)),
        [pltpu.VMEM],
        pieces,
        scratch_shapes=[pltpu.SMEM((MEMBERS, HD), jnp.int32), pltpu.SemaphoreType.DMA],
    )
    prompt_rows = over_pick(picked).reshape(2, KV_LANE, GROUPS, LOCAL, SLICE, HD)
    resp_key_grad, resp_value_grad, terms, probability, score_grad = attend(
        lengths, queries, out_grad, resp_keys, resp_values, prompt_rows
    )
    terms = over_pick(terms.reshape(MEMBERS, LOCAL, SLICE, HD))
    attn_out, query_grad, token = outputs(
        lengths, resp_keys, resp_values, prompt_rows, probability, score_grad, queries.shape[1]
    )
    sums = whole(
        fold_kernel,
        low(PROMPTS * LANES, TILE, HD),
        [pltpu.SMEM, pltpu.VMEM, pl.ANY],
        owners,
        terms,
        token,
        scratch_shapes=[pltpu.VMEM((PROMPTS, SLICE, HD), jnp.float32)],
    )
    prompt_key_grad, prompt_value_grad = whole(
        summed_kernel,
        (low(*prompt_keys.shape), low(*prompt_values.shape)),
        [pltpu.VMEM],
        over_store(sums),
    )
    return (
        attn_out,
        query_grad,
        resp_key_grad,
        resp_value_grad,
        prompt_key_grad,
        prompt_value_grad,
    )


def solution(mesh):
    wide = P("resp", "tp")
    stored = P(("resp", "tp"), None)
    return jax.shard_map(
        shards,
        mesh=mesh,
        in_specs=(wide, wide, wide, wide, stored, stored, P("resp"), P("resp")),
        out_specs=(wide, wide, wide, wide, stored, stored),
        check_vma=False,
    )
```

```python
import jax
import jax.numpy as jnp
from jax import lax
from jax.experimental import pallas as pl
from jax.experimental.pallas import tpu as pltpu
from jax.sharding import PartitionSpec as P

HD = 128
LP = 256
ROWS = 32
PER_GROUP = 8
KV_LANE = 2
LANES = 4
GROUPS = 4
TILE = 16
MEMBERS = 16
PROMPTS = 16
LOCAL = 4
SLICE = LP // GROUPS
CHUNKS = 5
SENT = TILE + 8
LOG2E = 1.4426950408889634
LARGE = pltpu.CompilerParams(vmem_limit_bytes=48 * 1024 * 1024)
FIRST = pltpu.CompilerParams(vmem_limit_bytes=(64 * 1024 - 64) * 1024)
SMALL = pltpu.CompilerParams(vmem_limit_bytes=16 * 1024 * 1024)

STORE_GROUPS = [
    [
        (z * 32 + x * 8 + high * 4 + (turn + t) % 4) * 4 + t
        for x in range(4)
        for t in range(LANES)
    ]
    for z in range(2)
    for high in range(2)
    for turn in range(4)
]
PICK_GROUPS = [
    [z * 32 + x * 8 + high * 4 + block for x in range(4) for block in range(4)]
    for z in range(2)
    for high in range(2)
]


def over_store(array):
    return lax.all_to_all(
        array,
        ("resp", "tp"),
        split_axis=0,
        concat_axis=0,
        tiled=True,
        axis_index_groups=STORE_GROUPS,
    )


def over_pick(array):
    return lax.all_to_all(
        array, "resp", split_axis=0, concat_axis=0, tiled=True, axis_index_groups=PICK_GROUPS
    )


FLIPS = (4, 32, 36)


def across(array, flip):
    return lax.ppermute(array, "resp", [(at, at ^ flip) for at in range(64)])


def corner():
    prompt = lax.axis_index("resp") // 4
    return prompt // 8, prompt % 2


def column_of(x):
    return (x // KV_LANE, x % KV_LANE)


def stored_kernel(
    owner_hbm, key_hbm, value_hbm, out_ref, owner_ref, key_ref, value_ref, sems
):
    copies = [
        pltpu.make_async_copy(source, target, sems.at[at])
        for at, (source, target) in enumerate(
            ((owner_hbm, owner_ref), (key_hbm, key_ref), (value_hbm, value_ref))
        )
    ]
    for copy in copies:
        copy.start()
    for copy in copies:
        copy.wait()
    at = lax.broadcasted_iota(jnp.int32, (SENT - TILE, HD), 1)
    asked = jnp.zeros((SENT - TILE, HD), jnp.int32)
    for one in range(LOCAL):
        asked = jnp.where(at == one, owner_ref[one], asked)
    asked = asked.astype(jnp.float32).astype(jnp.bfloat16)
    for x in range(4):
        which, head = column_of(x)
        source = value_ref if which else key_ref
        for lane in range(LANES):
            first = (lane * KV_LANE + head) * HD
            out_ref[x * LANES + lane] = jnp.concatenate(
                [source[:, first : first + HD], asked], 0
            )


def asked_kernel(pieces_ref, out_ref, owner_ref):
    turn = (lax.axis_index("resp") % 4 + LANES - lax.axis_index("tp")) % 4
    for x in range(4):
        for block in range(4):
            tile = pieces_ref[x * LANES + (block + 4 - turn) % 4].astype(jnp.float32)
            owner_ref[x * 4 + block : x * 4 + block + 1] = tile[TILE : TILE + 1].astype(jnp.int32)
    for member in range(MEMBERS):
        out_ref[member] = pieces_ref[member, :TILE]


def pick_kernel(owner_ref, own_ref, first_ref, second_ref, third_ref, out_ref, table):
    z, high = corner()
    for flip, part_ref in enumerate((own_ref, first_ref, second_ref, third_ref)):
        for member in range(MEMBERS):
            table[flip * MEMBERS + member] = part_ref[member]
    for member in range(MEMBERS):
        for one in range(LOCAL):
            owner = owner_ref[member, one]
            flip = (owner // 8 + z) % 2 * 2 + (owner + high) % 2
            source = flip * MEMBERS + owner // 2 % 4 * LANES
            for lane in range(LANES):
                out_ref[member, one, lane * TILE : (lane + 1) * TILE] = table[source + lane]


def fold_kernel(
    owner_ref, terms_ref, token_ref, own_ref, first_ref, second_ref, third_ref, total
):
    z, high = corner()
    total[...] = jnp.zeros_like(total)
    for one in range(LOCAL):
        for member in range(MEMBERS):
            owner = owner_ref[member, one]
            total[owner] += terms_ref[member, one].astype(jnp.float32)
    for flip, out_ref in enumerate((own_ref, first_ref, second_ref, third_ref)):
        for x in range(4):
            prompt = (z + flip // 2) % 2 * 8 + x * 2 + (high + flip) % 2
            for lane in range(LANES):
                out_ref[x * LANES + lane] = total[
                    prompt, lane * TILE : (lane + 1) * TILE
                ].astype(out_ref.dtype)


def sum_kernel(own_ref, first_ref, second_ref, third_ref, out_ref):
    for member in range(MEMBERS):
        tile = own_ref[member]
        for part_ref in (first_ref, second_ref, third_ref):
            tile = tile + part_ref[member].astype(jnp.float32)
        out_ref[member] = tile.astype(out_ref.dtype)


def place_kernel(sums_ref, key_ref, value_ref):
    for x in range(4):
        which, head = column_of(x)
        target = value_ref if which else key_ref
        for lane in range(LANES):
            first = (lane * KV_LANE + head) * HD
            target[:, first : first + HD] = sums_ref[x * LANES + lane]


def heads(head):
    for at in range(PER_GROUP):
        column = (head * PER_GROUP + at) * HD
        yield slice(at * ROWS, (at + 1) * ROWS), slice(column, column + HD)


def by_length(length, span, work, blank):
    for first in range(0, span, 2 * ROWS):
        second = first + ROWS
        last = min(second + ROWS, span)
        if second < span:

            @pl.when(length > second)
            def _():
                work((first, second))

        @pl.when((length > first) & ((length <= second) | (second >= span)))
        def _():
            work((first,))
            if second < span:
                blank(second, last)

        @pl.when(length <= first)
        def _():
            blank(first, last)


def attend_kernel(
    length_ref,
    query_ref,
    grad_ref,
    key_ref,
    value_ref,
    prompt_ref,
    key_grad_ref,
    value_grad_ref,
    prompt_grad_ref,
    probability_ref,
    score_grad_ref,
    keys,
    values,
    stacked_query,
    stacked_grad,
    scores,
    prob_grads,
    key_total,
    value_total,
):
    length = length_ref[pl.program_id(0)]
    span = query_ref.shape[0]
    scale = HD**-0.5
    wide = PER_GROUP * ROWS
    for head in range(KV_LANE):
        for whole, own_ref, which in ((keys, key_ref, 0), (values, value_ref, 1)):
            whole[head, :LP] = prompt_ref[which, head, :, 0].reshape(LP, HD)
            whole[head, LP:] = own_ref[:, head * HD : (head + 1) * HD]

    def score(slot, head, first):
        count = LP + first + ROWS
        lane = lax.broadcasted_iota(jnp.int32, (1, wide), 1) % ROWS
        causal = lax.broadcasted_iota(jnp.int32, (ROWS, 1), 0) <= lane
        for part, column in heads(head):
            stacked_query[slot, part] = query_ref[first : first + ROWS, column]
            stacked_grad[slot, part] = grad_ref[first : first + ROWS, column]
        raw = lax.dot_general(
            keys[head, :count],
            stacked_query[slot],
            (((1,), (1,)), ((), ())),
            preferred_element_type=jnp.float32,
        )
        tail = jnp.where(causal, raw[count - ROWS :], -1e30)
        scores[slot, : count - ROWS] = raw[: count - ROWS]
        scores[slot, count - ROWS : count] = tail
        top = jnp.max(raw[: count - ROWS].reshape(-1, 8, wide), axis=0)
        top = jnp.maximum(top, jnp.max(tail.reshape(-1, 8, wide), axis=0))
        prob_grads[slot, :count] = lax.dot_general(
            values[head, :count],
            stacked_grad[slot],
            (((1,), (1,)), ((), ())),
            preferred_element_type=jnp.float32,
        )
        return jnp.max(top, axis=0, keepdims=True) * (scale * LOG2E)

    def soften(slot, head, first, largest):
        count = LP + first + ROWS
        chunk = first // ROWS
        lane = lax.broadcasted_iota(jnp.int32, (1, wide), 1) % ROWS
        live = first + lane < length
        blocks = [slice(at, at + ROWS) for at in range(0, count, ROWS)]
        total = jnp.zeros((8, wide), jnp.float32)
        moved = jnp.zeros((8, wide), jnp.float32)
        for block in blocks:
            weights = jnp.exp2(scores[slot, block] * (scale * LOG2E) - largest)
            scores[slot, block] = weights
            total = total + jnp.sum(weights.reshape(-1, 8, wide), axis=0)
            terms = weights * prob_grads[slot, block]
            moved = moved + jnp.sum(terms.reshape(-1, 8, wide), axis=0)
        inverse = jnp.where(live, 1.0 / jnp.sum(total, axis=0, keepdims=True), 0.0)
        delta = jnp.sum(moved, axis=0, keepdims=True) * inverse
        for block in blocks:
            probability = scores[slot, block] * inverse
            probability_ref[0, head, chunk, block] = probability.astype(jnp.bfloat16)
            score_grad_ref[0, head, chunk, block] = (
                probability * (prob_grads[slot, block] - delta)
            ).astype(jnp.bfloat16)

    def gather(slot, head, first):
        count = LP + first + ROWS
        chunk = first // ROWS
        for total, left_ref, stacked in (
            (value_total, probability_ref, stacked_grad),
            (key_total, score_grad_ref, stacked_query),
        ):
            terms = jnp.dot(
                left_ref[0, head, chunk, :count],
                stacked[slot],
                preferred_element_type=jnp.float32,
            )
            if first == 0:
                total[head, :count] = terms
            else:
                total[head, : count - ROWS] += terms[: count - ROWS]
                total[head, count - ROWS : count] = terms[count - ROWS :]

    def work(firsts):
        streams = [(head, first) for first in firsts for head in range(KV_LANE)]
        largest = {0: score(0, *streams[0])}
        for slot, stream in enumerate(streams):
            if slot + 1 < len(streams):
                largest[slot + 1] = score(slot + 1, *streams[slot + 1])
            soften(slot, *stream, largest[slot])
            gather(slot, *stream)

    def blank(first, last):
        zeros = jnp.zeros((KV_LANE, last - first, HD), jnp.float32)
        key_total[:, LP + first : LP + last] = zeros
        value_total[:, LP + first : LP + last] = zeros

    by_length(length, span, work, blank)

    for head in range(KV_LANE):
        lanes = slice(head * HD, (head + 1) * HD)
        key_terms = (key_total[head] * scale).astype(jnp.bfloat16)
        value_terms = value_total[head].astype(jnp.bfloat16)
        prompt_grad_ref[0, head, :, 0] = key_terms[:LP].reshape(GROUPS, SLICE, HD)
        prompt_grad_ref[1, head, :, 0] = value_terms[:LP].reshape(GROUPS, SLICE, HD)
        key_grad_ref[:, lanes] = key_terms[LP:]
        value_grad_ref[:, lanes] = value_terms[LP:]


def outputs_kernel(
    length_ref,
    key_ref,
    value_ref,
    prompt_ref,
    probability_ref,
    score_grad_ref,
    out_ref,
    query_grad_ref,
    token_ref,
    keys_t,
    values_t,
):
    length = length_ref[pl.program_id(0)]
    span = out_ref.shape[0]
    scale = HD**-0.5
    for head in range(KV_LANE):
        lanes = slice(head * HD, (head + 1) * HD)
        for whole_t, own_ref, which in ((keys_t, key_ref, 0), (values_t, value_ref, 1)):
            whole_t[head] = jnp.concatenate(
                [prompt_ref[which, head, :, 0].reshape(LP, HD), own_ref[:, lanes]], 0
            ).T

    def work(firsts):
        for first in firsts:
            count = LP + first + ROWS
            chunk = first // ROWS
            rows = slice(first, first + ROWS)
            for head in range(KV_LANE):
                output = jnp.dot(
                    values_t[head, :, :count],
                    probability_ref[0, head, chunk, :count],
                    preferred_element_type=jnp.float32,
                )
                query_grad = jnp.dot(
                    keys_t[head, :, :count],
                    score_grad_ref[0, head, chunk, :count],
                    preferred_element_type=jnp.float32,
                )
                output = output.astype(jnp.bfloat16).T
                query_grad = (query_grad * scale).astype(jnp.bfloat16).T
                for part, column in heads(head):
                    out_ref[rows, column] = output[part]
                    query_grad_ref[rows, column] = query_grad[part]

    def blank(first, last):
        zeros = jnp.zeros((last - first, out_ref.shape[1]), jnp.bfloat16)
        out_ref[first:last, :] = zeros
        query_grad_ref[first:last, :] = zeros

    by_length(length, span, work, blank)
    token_ref[...] = jnp.zeros_like(token_ref)


def specs(span, wide, narrow):
    both = LP + span
    stacked = PER_GROUP * ROWS
    return dict(
        wide=pl.BlockSpec((span, wide), lambda i, length: (i, 0)),
        narrow=pl.BlockSpec((span, narrow), lambda i, length: (i, 0)),
        prompt=pl.BlockSpec(
            (2, KV_LANE, GROUPS, 1, SLICE, HD), lambda i, length: (0, 0, 0, i, 0, 0)
        ),
        kept=pl.BlockSpec(
            (1, KV_LANE, CHUNKS, both, stacked), lambda i, length: (i, 0, 0, 0, 0)
        ),
    )


def attend(lengths, queries, out_grad, resp_keys, resp_values, prompt_rows):
    count = lengths.shape[0]
    span = queries.shape[0] // count
    both = LP + span
    streams = 2 * KV_LANE
    stacked = PER_GROUP * ROWS
    spec = specs(span, queries.shape[1], resp_keys.shape[1])
    kept = jax.ShapeDtypeStruct((count, KV_LANE, CHUNKS, both, stacked), jnp.bfloat16)
    return pl.pallas_call(
        attend_kernel,
        out_shape=(
            jax.ShapeDtypeStruct(resp_keys.shape, jnp.bfloat16),
            jax.ShapeDtypeStruct(resp_keys.shape, jnp.bfloat16),
            jax.ShapeDtypeStruct(prompt_rows.shape, jnp.bfloat16),
            kept,
            kept,
        ),
        grid_spec=pltpu.PrefetchScalarGridSpec(
            num_scalar_prefetch=1,
            grid=(count,),
            in_specs=[spec[name] for name in ("wide", "wide", "narrow", "narrow", "prompt")],
            out_specs=[spec[name] for name in ("narrow", "narrow", "prompt", "kept", "kept")],
            scratch_shapes=[
                pltpu.VMEM((KV_LANE, both, HD), jnp.bfloat16),
                pltpu.VMEM((KV_LANE, both, HD), jnp.bfloat16),
                pltpu.VMEM((streams, stacked, HD), jnp.bfloat16),
                pltpu.VMEM((streams, stacked, HD), jnp.bfloat16),
                pltpu.VMEM((streams, both, stacked), jnp.float32),
                pltpu.VMEM((streams, both, stacked), jnp.float32),
                pltpu.VMEM((KV_LANE, both, HD), jnp.float32),
                pltpu.VMEM((KV_LANE, both, HD), jnp.float32),
            ],
        ),
        compiler_params=LARGE,
        cost_estimate=pl.CostEstimate(
            flops=16 * queries.size * both,
            bytes_accessed=4 * queries.size,
            transcendentals=queries.size * both // HD,
        ),
    )(lengths, queries, out_grad, resp_keys, resp_values, prompt_rows)


def outputs(lengths, resp_keys, resp_values, prompt_rows, probability, score_grad, wide):
    count = lengths.shape[0]
    rows = resp_keys.shape[0]
    span = rows // count
    both = LP + span
    spec = specs(span, wide, resp_keys.shape[1])
    shape = jax.ShapeDtypeStruct((rows, wide), jnp.bfloat16)
    return pl.pallas_call(
        outputs_kernel,
        out_shape=(shape, shape, jax.ShapeDtypeStruct((8, HD), jnp.int32)),
        grid_spec=pltpu.PrefetchScalarGridSpec(
            num_scalar_prefetch=1,
            grid=(count,),
            in_specs=[spec[name] for name in ("narrow", "narrow", "prompt", "kept", "kept")],
            out_specs=[
                spec["wide"],
                spec["wide"],
                pl.BlockSpec((8, HD), lambda i, length: (0, 0)),
            ],
            scratch_shapes=[
                pltpu.VMEM((KV_LANE, HD, both), jnp.bfloat16),
                pltpu.VMEM((KV_LANE, HD, both), jnp.bfloat16),
            ],
        ),
        compiler_params=LARGE,
        cost_estimate=pl.CostEstimate(
            flops=8 * rows * wide * both,
            bytes_accessed=4 * rows * wide + 4 * probability.size,
            transcendentals=0,
        ),
    )(lengths, resp_keys, resp_values, prompt_rows, probability, score_grad)


def whole(kernel, out_shape, spaces, *operands, params=SMALL, **more):
    return pl.pallas_call(
        kernel,
        out_shape=out_shape,
        in_specs=[pl.BlockSpec(memory_space=space) for space in spaces],
        compiler_params=params,
        **more,
    )(*operands)


def low(*shape):
    return jax.ShapeDtypeStruct(shape, jnp.bfloat16)


def shards(
    queries, resp_keys, resp_values, out_grad, prompt_keys, prompt_values, lengths, prompt_of
):
    pieces = over_store(
        whole(
            stored_kernel,
            low(MEMBERS, SENT, HD),
            [pltpu.HBM] * 3,
            prompt_of,
            prompt_keys,
            prompt_values,
            params=FIRST,
            scratch_shapes=[
                pltpu.SMEM(prompt_of.shape, jnp.int32),
                pltpu.VMEM(prompt_keys.shape, jnp.bfloat16),
                pltpu.VMEM(prompt_values.shape, jnp.bfloat16),
                pltpu.SemaphoreType.DMA((3,)),
            ],
        )
    )
    part = (MEMBERS, TILE, HD)
    own, owners = whole(
        asked_kernel,
        (low(*part), jax.ShapeDtypeStruct((MEMBERS, HD), jnp.int32)),
        [pltpu.VMEM],
        pieces,
    )
    picked = whole(
        pick_kernel,
        low(MEMBERS, LOCAL, SLICE, HD),
        [pltpu.SMEM] + [pltpu.VMEM] * 4,
        owners,
        own,
        *(across(own, flip) for flip in FLIPS),
        scratch_shapes=[pltpu.VMEM((PROMPTS * LANES, TILE, HD), jnp.bfloat16)],
    )
    prompt_rows = over_pick(picked).reshape(2, KV_LANE, GROUPS, LOCAL, SLICE, HD)
    resp_key_grad, resp_value_grad, terms, probability, score_grad = attend(
        lengths, queries, out_grad, resp_keys, resp_values, prompt_rows
    )
    terms = over_pick(terms.reshape(MEMBERS, LOCAL, SLICE, HD))
    attn_out, query_grad, token = outputs(
        lengths, resp_keys, resp_values, prompt_rows, probability, score_grad, queries.shape[1]
    )
    own, *others = whole(
        fold_kernel,
        (jax.ShapeDtypeStruct(part, jnp.float32),) + (low(*part),) * 3,
        [pltpu.SMEM, pltpu.VMEM, pl.ANY],
        owners,
        terms,
        token,
        scratch_shapes=[pltpu.VMEM((PROMPTS, SLICE, HD), jnp.float32)],
    )
    others = [across(other, flip) for other, flip in zip(others, FLIPS)]
    sums = whole(sum_kernel, low(*part), [pltpu.VMEM] * 4, own, *others)
    prompt_key_grad, prompt_value_grad = whole(
        place_kernel,
        (low(*prompt_keys.shape), low(*prompt_values.shape)),
        [pltpu.VMEM],
        over_store(sums),
    )
    return (
        attn_out,
        query_grad,
        resp_key_grad,
        resp_value_grad,
        prompt_key_grad,
        prompt_value_grad,
    )


def solution(mesh):
    wide = P("resp", "tp")
    stored = P(("resp", "tp"), None)
    return jax.shard_map(
        shards,
        mesh=mesh,
        in_specs=(wide, wide, wide, wide, stored, stored, P("resp"), P("resp")),
        out_specs=(wide, wide, wide, wide, stored, stored),
        check_vma=False,
    )
```

```python
import jax
import jax.numpy as jnp
from jax import lax
from jax.experimental import pallas as pl
from jax.experimental.pallas import tpu as pltpu
from jax.sharding import PartitionSpec as P

HD = 128
LP = 256
ROWS = 32
PER_GROUP = 8
KV_LANE = 2
LANES = 4
GROUPS = 4
TILE = 16
MEMBERS = 16
PROMPTS = 16
LOCAL = 4
SLICE = LP // GROUPS
CHUNKS = 5
SENT = TILE + 8
LOG2E = 1.4426950408889634
LARGE = pltpu.CompilerParams(vmem_limit_bytes=24 * 1024 * 1024)
FIRST = pltpu.CompilerParams(vmem_limit_bytes=(64 * 1024 - 64) * 1024)
STACK = pltpu.CompilerParams(vmem_limit_bytes=55 * 1024 * 1024)
SMALL = pltpu.CompilerParams(vmem_limit_bytes=16 * 1024 * 1024)

STORE_GROUPS = [
    [(p * 4 + (turn + t) % 4) * 4 + t for p in range(PROMPTS) for t in range(LANES)]
    for turn in range(4)
]
PICK_GROUPS = [
    [z * 32 + x * 8 + high * 4 + block for x in range(4) for block in range(4)]
    for z in range(2)
    for high in range(2)
]


def over_store(array):
    return lax.all_to_all(
        array,
        ("resp", "tp"),
        split_axis=0,
        concat_axis=0,
        tiled=True,
        axis_index_groups=STORE_GROUPS,
    )


def over_pick(array):
    return lax.all_to_all(
        array, "resp", split_axis=0, concat_axis=0, tiled=True, axis_index_groups=PICK_GROUPS
    )


def column_of(x):
    return (x // KV_LANE, x % KV_LANE)


def stored_kernel(
    owner_hbm, key_hbm, value_hbm, out_ref, owner_ref, key_ref, value_ref, sems
):
    copies = [
        pltpu.make_async_copy(source, target, sems.at[at])
        for at, (source, target) in enumerate(
            ((owner_hbm, owner_ref), (key_hbm, key_ref), (value_hbm, value_ref))
        )
    ]
    for copy in copies:
        copy.start()
    for copy in copies:
        copy.wait()
    at = lax.broadcasted_iota(jnp.int32, (SENT - TILE, HD), 1)
    asked = jnp.zeros((SENT - TILE, HD), jnp.int32)
    for one in range(LOCAL):
        asked = jnp.where(at == one, owner_ref[one], asked)
    asked = asked.astype(jnp.float32).astype(jnp.bfloat16)
    for prompt in range(PROMPTS):
        which, head = column_of(prompt // 2 % 4)
        source = value_ref if which else key_ref
        for lane in range(LANES):
            first = (lane * KV_LANE + head) * HD
            out_ref[prompt * LANES + lane] = jnp.concatenate(
                [source[:, first : first + HD], asked], 0
            )


def pick_kernel(pieces_ref, out_ref, owner_ref, owners, sem):
    resp = lax.axis_index("resp")
    prompt = resp // 4
    turn = (resp % 4 + LANES - lax.axis_index("tp")) % 4
    for x in range(4):
        for block in range(4):
            source = (prompt // 8 * 8 + x * 2 + prompt % 2) * LANES + (block + 4 - turn) % 4
            tile = pieces_ref[source].astype(jnp.float32)
            owner_ref[x * 4 + block : x * 4 + block + 1] = tile[TILE : TILE + 1].astype(jnp.int32)
    copy = pltpu.make_async_copy(owner_ref, owners, sem)
    copy.start()
    copy.wait()
    for member in range(MEMBERS):
        for one in range(LOCAL):
            owner = owners[member, one]
            for lane in range(LANES):
                out_ref[member, one, lane * TILE : (lane + 1) * TILE] = pieces_ref[
                    owner * LANES + lane, :TILE
                ]


def fold_kernel(owner_ref, terms_ref, token_ref, out_ref, total):
    total[...] = jnp.zeros_like(total)
    for one in range(LOCAL):
        for member in range(MEMBERS):
            owner = owner_ref[member, one]
            total[owner] += terms_ref[member, one].astype(jnp.float32)
    for prompt in range(PROMPTS):
        for lane in range(LANES):
            out_ref[prompt * LANES + lane] = total[
                prompt, lane * TILE : (lane + 1) * TILE
            ].astype(out_ref.dtype)


def summed_kernel(sums_ref, key_ref, value_ref):
    for x in range(4):
        which, head = column_of(x)
        target = value_ref if which else key_ref
        for lane in range(LANES):
            tile = jnp.zeros((TILE, HD), jnp.float32)
            for z in range(2):
                for high in range(2):
                    source = (z * 8 + x * 2 + high) * LANES + lane
                    tile = tile + sums_ref[source].astype(jnp.float32)
            first = (lane * KV_LANE + head) * HD
            target[:, first : first + HD] = tile.astype(target.dtype)


def heads(head):
    for at in range(PER_GROUP):
        column = (head * PER_GROUP + at) * HD
        yield slice(at * ROWS, (at + 1) * ROWS), slice(column, column + HD)


def by_length(length, span, work, blank):
    for first in range(0, span, 2 * ROWS):
        second = first + ROWS
        last = min(second + ROWS, span)
        if second < span:

            @pl.when(length > second)
            def _():
                work((first, second))

        @pl.when((length > first) & ((length <= second) | (second >= span)))
        def _():
            work((first,))
            if second < span:
                blank(second, last)

        @pl.when(length <= first)
        def _():
            blank(first, last)


def stack_kernel(query_ref, grad_ref, stacked_query, stacked_grad):
    response = pl.program_id(0)
    for chunk in range(CHUNKS):
        rows = slice(chunk * ROWS, (chunk + 1) * ROWS)
        for head in range(KV_LANE):
            for part, column in heads(head):
                stacked_query[response, head, chunk, part] = query_ref[rows, column]
                stacked_grad[response, head, chunk, part] = grad_ref[rows, column]


def attend_kernel(
    length_ref,
    stacked_query,
    stacked_grad,
    key_ref,
    value_ref,
    prompt_ref,
    key_grad_ref,
    value_grad_ref,
    prompt_grad_ref,
    probability_ref,
    score_grad_ref,
    keys,
    values,
    scores,
    prob_grads,
    key_total,
    value_total,
):
    response = pl.program_id(0)
    length = length_ref[response]
    span = key_ref.shape[0]
    scale = HD**-0.5
    wide = PER_GROUP * ROWS
    for head in range(KV_LANE):
        for whole, own_ref, which in ((keys, key_ref, 0), (values, value_ref, 1)):
            whole[head, :LP] = prompt_ref[which, head, :, 0].reshape(LP, HD)
            whole[head, LP:] = own_ref[:, head * HD : (head + 1) * HD]

    def score(slot, head, first):
        count = LP + first + ROWS
        lane = lax.broadcasted_iota(jnp.int32, (1, wide), 1) % ROWS
        causal = lax.broadcasted_iota(jnp.int32, (ROWS, 1), 0) <= lane
        raw = lax.dot_general(
            keys[head, :count],
            stacked_query[response, head, first // ROWS],
            (((1,), (1,)), ((), ())),
            preferred_element_type=jnp.float32,
        )
        tail = jnp.where(causal, raw[count - ROWS :], -1e30)
        scores[slot, : count - ROWS] = raw[: count - ROWS]
        scores[slot, count - ROWS : count] = tail
        top = jnp.max(raw[: count - ROWS].reshape(-1, 8, wide), axis=0)
        top = jnp.maximum(top, jnp.max(tail.reshape(-1, 8, wide), axis=0))
        prob_grads[slot, :count] = lax.dot_general(
            values[head, :count],
            stacked_grad[response, head, first // ROWS],
            (((1,), (1,)), ((), ())),
            preferred_element_type=jnp.float32,
        )
        return jnp.max(top, axis=0, keepdims=True) * (scale * LOG2E)

    def soften(slot, head, first, largest):
        count = LP + first + ROWS
        chunk = first // ROWS
        lane = lax.broadcasted_iota(jnp.int32, (1, wide), 1) % ROWS
        live = first + lane < length
        blocks = [slice(at, at + ROWS) for at in range(0, count, ROWS)]
        total = jnp.zeros((8, wide), jnp.float32)
        moved = jnp.zeros((8, wide), jnp.float32)
        for block in blocks:
            weights = jnp.exp2(scores[slot, block] * (scale * LOG2E) - largest)
            scores[slot, block] = weights
            total = total + jnp.sum(weights.reshape(-1, 8, wide), axis=0)
            terms = weights * prob_grads[slot, block]
            moved = moved + jnp.sum(terms.reshape(-1, 8, wide), axis=0)
        inverse = jnp.where(live, 1.0 / jnp.sum(total, axis=0, keepdims=True), 0.0)
        delta = jnp.sum(moved, axis=0, keepdims=True) * inverse
        for block in blocks:
            probability = scores[slot, block] * inverse
            probability_ref[response, head, chunk, block] = probability.astype(jnp.bfloat16)
            score_grad_ref[response, head, chunk, block] = (
                probability * (prob_grads[slot, block] - delta)
            ).astype(jnp.bfloat16)

    def gather(slot, head, first):
        count = LP + first + ROWS
        chunk = first // ROWS
        for total, left_ref, stacked in (
            (value_total, probability_ref, stacked_grad),
            (key_total, score_grad_ref, stacked_query),
        ):
            terms = jnp.dot(
                left_ref[response, head, chunk, :count],
                stacked[response, head, chunk],
                preferred_element_type=jnp.float32,
            )
            if first == 0:
                total[head, :count] = terms
            else:
                total[head, : count - ROWS] += terms[: count - ROWS]
                total[head, count - ROWS : count] = terms[count - ROWS :]

    def work(firsts):
        streams = [(head, first) for first in firsts for head in range(KV_LANE)]
        largest = {0: score(0, *streams[0])}
        for slot, stream in enumerate(streams):
            if slot + 1 < len(streams):
                largest[slot + 1] = score(slot + 1, *streams[slot + 1])
            soften(slot, *stream, largest[slot])
            gather(slot, *stream)

    def blank(first, last):
        zeros = jnp.zeros((KV_LANE, last - first, HD), jnp.float32)
        key_total[:, LP + first : LP + last] = zeros
        value_total[:, LP + first : LP + last] = zeros

    by_length(length, span, work, blank)

    for head in range(KV_LANE):
        lanes = slice(head * HD, (head + 1) * HD)
        key_terms = (key_total[head] * scale).astype(jnp.bfloat16)
        value_terms = value_total[head].astype(jnp.bfloat16)
        prompt_grad_ref[0, head, :, 0] = key_terms[:LP].reshape(GROUPS, SLICE, HD)
        prompt_grad_ref[1, head, :, 0] = value_terms[:LP].reshape(GROUPS, SLICE, HD)
        key_grad_ref[:, lanes] = key_terms[LP:]
        value_grad_ref[:, lanes] = value_terms[LP:]


def outputs_kernel(
    length_ref,
    key_ref,
    value_ref,
    prompt_ref,
    probability_ref,
    score_grad_ref,
    out_ref,
    query_grad_ref,
    token_ref,
    keys_t,
    values_t,
):
    response = pl.program_id(0)
    length = length_ref[response]
    span = out_ref.shape[0]
    scale = HD**-0.5
    for head in range(KV_LANE):
        lanes = slice(head * HD, (head + 1) * HD)
        for whole_t, own_ref, which in ((keys_t, key_ref, 0), (values_t, value_ref, 1)):
            whole_t[head] = jnp.concatenate(
                [prompt_ref[which, head, :, 0].reshape(LP, HD), own_ref[:, lanes]], 0
            ).T

    def work(firsts):
        for first in firsts:
            count = LP + first + ROWS
            chunk = first // ROWS
            rows = slice(first, first + ROWS)
            for head in range(KV_LANE):
                output = jnp.dot(
                    values_t[head, :, :count],
                    probability_ref[response, head, chunk, :count],
                    preferred_element_type=jnp.float32,
                )
                query_grad = jnp.dot(
                    keys_t[head, :, :count],
                    score_grad_ref[response, head, chunk, :count],
                    preferred_element_type=jnp.float32,
                )
                output = output.astype(jnp.bfloat16).T
                query_grad = (query_grad * scale).astype(jnp.bfloat16).T
                for part, column in heads(head):
                    out_ref[rows, column] = output[part]
                    query_grad_ref[rows, column] = query_grad[part]

    def blank(first, last):
        zeros = jnp.zeros((last - first, out_ref.shape[1]), jnp.bfloat16)
        out_ref[first:last, :] = zeros
        query_grad_ref[first:last, :] = zeros

    by_length(length, span, work, blank)
    token_ref[...] = jnp.zeros_like(token_ref)


def specs(span, wide, narrow):
    return dict(
        wide=pl.BlockSpec((span, wide), lambda i, length: (i, 0)),
        narrow=pl.BlockSpec((span, narrow), lambda i, length: (i, 0)),
        prompt=pl.BlockSpec(
            (2, KV_LANE, GROUPS, 1, SLICE, HD), lambda i, length: (0, 0, 0, i, 0, 0)
        ),
        kept=pl.BlockSpec(memory_space=pltpu.VMEM),
    )


def stack(queries, out_grad, count):
    span = queries.shape[0] // count
    shape = jax.ShapeDtypeStruct(
        (count, KV_LANE, CHUNKS, PER_GROUP * ROWS, HD), jnp.bfloat16
    )
    wide = pl.BlockSpec((span, queries.shape[1]), lambda i: (i, 0))
    return pl.pallas_call(
        stack_kernel,
        out_shape=(shape, shape),
        grid=(count,),
        in_specs=[wide, wide],
        out_specs=[pl.BlockSpec(memory_space=pltpu.VMEM)] * 2,
        compiler_params=STACK,
        cost_estimate=pl.CostEstimate(
            flops=0, bytes_accessed=8 * queries.size, transcendentals=0
        ),
    )(queries, out_grad)


def attend(lengths, stacked_query, stacked_grad, resp_keys, resp_values, prompt_rows):
    count = lengths.shape[0]
    span = resp_keys.shape[0] // count
    both = LP + span
    streams = 2 * KV_LANE
    stacked = PER_GROUP * ROWS
    elements = stacked_query.size
    spec = specs(span, stacked_query.size // resp_keys.shape[0], resp_keys.shape[1])
    kept = jax.ShapeDtypeStruct((count, KV_LANE, CHUNKS, both, stacked), jnp.bfloat16)
    return pl.pallas_call(
        attend_kernel,
        out_shape=(
            jax.ShapeDtypeStruct(resp_keys.shape, jnp.bfloat16),
            jax.ShapeDtypeStruct(resp_keys.shape, jnp.bfloat16),
            jax.ShapeDtypeStruct(prompt_rows.shape, jnp.bfloat16),
            kept,
            kept,
        ),
        grid_spec=pltpu.PrefetchScalarGridSpec(
            num_scalar_prefetch=1,
            grid=(count,),
            in_specs=[spec[name] for name in ("kept", "kept", "narrow", "narrow", "prompt")],
            out_specs=[spec[name] for name in ("narrow", "narrow", "prompt", "kept", "kept")],
            scratch_shapes=[
                pltpu.VMEM((KV_LANE, both, HD), jnp.bfloat16),
                pltpu.VMEM((KV_LANE, both, HD), jnp.bfloat16),
                pltpu.VMEM((streams, both, stacked), jnp.float32),
                pltpu.VMEM((streams, both, stacked), jnp.float32),
                pltpu.VMEM((KV_LANE, both, HD), jnp.float32),
                pltpu.VMEM((KV_LANE, both, HD), jnp.float32),
            ],
        ),
        compiler_params=LARGE,
        cost_estimate=pl.CostEstimate(
            flops=16 * elements * both,
            bytes_accessed=4 * elements,
            transcendentals=elements * both // HD,
        ),
    )(lengths, stacked_query, stacked_grad, resp_keys, resp_values, prompt_rows)


def outputs(lengths, resp_keys, resp_values, prompt_rows, probability, score_grad, wide):
    count = lengths.shape[0]
    rows = resp_keys.shape[0]
    span = rows // count
    both = LP + span
    spec = specs(span, wide, resp_keys.shape[1])
    shape = jax.ShapeDtypeStruct((rows, wide), jnp.bfloat16)
    return pl.pallas_call(
        outputs_kernel,
        out_shape=(shape, shape, jax.ShapeDtypeStruct((8, HD), jnp.int32)),
        grid_spec=pltpu.PrefetchScalarGridSpec(
            num_scalar_prefetch=1,
            grid=(count,),
            in_specs=[spec[name] for name in ("narrow", "narrow", "prompt", "kept", "kept")],
            out_specs=[
                spec["wide"],
                spec["wide"],
                pl.BlockSpec((8, HD), lambda i, length: (0, 0)),
            ],
            scratch_shapes=[
                pltpu.VMEM((KV_LANE, HD, both), jnp.bfloat16),
                pltpu.VMEM((KV_LANE, HD, both), jnp.bfloat16),
            ],
        ),
        compiler_params=LARGE,
        cost_estimate=pl.CostEstimate(
            flops=8 * rows * wide * both,
            bytes_accessed=4 * rows * wide + 4 * probability.size,
            transcendentals=0,
        ),
    )(lengths, resp_keys, resp_values, prompt_rows, probability, score_grad)


def whole(kernel, out_shape, spaces, *operands, params=SMALL, **more):
    return pl.pallas_call(
        kernel,
        out_shape=out_shape,
        in_specs=[pl.BlockSpec(memory_space=space) for space in spaces],
        compiler_params=params,
        **more,
    )(*operands)


def low(*shape):
    return jax.ShapeDtypeStruct(shape, jnp.bfloat16)


def shards(
    queries, resp_keys, resp_values, out_grad, prompt_keys, prompt_values, lengths, prompt_of
):
    pieces = over_store(
        whole(
            stored_kernel,
            low(PROMPTS * LANES, SENT, HD),
            [pltpu.HBM] * 3,
            prompt_of,
            prompt_keys,
            prompt_values,
            params=FIRST,
            scratch_shapes=[
                pltpu.SMEM(prompt_of.shape, jnp.int32),
                pltpu.VMEM(prompt_keys.shape, jnp.bfloat16),
                pltpu.VMEM(prompt_values.shape, jnp.bfloat16),
                pltpu.SemaphoreType.DMA((3,)),
            ],
        )
    )
    picked, owners = whole(
        pick_kernel,
        (low(MEMBERS, LOCAL, SLICE, HD), jax.ShapeDtypeStruct((MEMBERS, HD), jnp.int32)),
        [pltpu.VMEM],
        pieces,
        scratch_shapes=[pltpu.SMEM((MEMBERS, HD), jnp.int32), pltpu.SemaphoreType.DMA],
    )
    prompt_rows = over_pick(picked).reshape(2, KV_LANE, GROUPS, LOCAL, SLICE, HD)
    stacked = stack(queries, out_grad, lengths.shape[0])
    resp_key_grad, resp_value_grad, terms, probability, score_grad = attend(
        lengths, *stacked, resp_keys, resp_values, prompt_rows
    )
    terms = over_pick(terms.reshape(MEMBERS, LOCAL, SLICE, HD))
    attn_out, query_grad, token = outputs(
        lengths, resp_keys, resp_values, prompt_rows, probability, score_grad, queries.shape[1]
    )
    sums = whole(
        fold_kernel,
        low(PROMPTS * LANES, TILE, HD),
        [pltpu.SMEM, pltpu.VMEM, pl.ANY],
        owners,
        terms,
        token,
        scratch_shapes=[pltpu.VMEM((PROMPTS, SLICE, HD), jnp.float32)],
    )
    prompt_key_grad, prompt_value_grad = whole(
        summed_kernel,
        (low(*prompt_keys.shape), low(*prompt_values.shape)),
        [pltpu.VMEM],
        over_store(sums),
    )
    return (
        attn_out,
        query_grad,
        resp_key_grad,
        resp_value_grad,
        prompt_key_grad,
        prompt_value_grad,
    )


def solution(mesh):
    wide = P("resp", "tp")
    stored = P(("resp", "tp"), None)
    return jax.shard_map(
        shards,
        mesh=mesh,
        in_specs=(wide, wide, wide, wide, stored, stored, P("resp"), P("resp")),
        out_specs=(wide, wide, wide, wide, stored, stored),
        check_vma=False,
    )
```

```python
import jax
import jax.numpy as jnp
from jax import lax
from jax.experimental import pallas as pl
from jax.experimental.pallas import tpu as pltpu
from jax.sharding import PartitionSpec as P

HD = 128
LP = 256
ROWS = 32
PER_GROUP = 8
KV_LANE = 2
LANES = 4
GROUPS = 4
TILE = 16
MEMBERS = 16
PROMPTS = 16
LOCAL = 4
SLICE = LP // GROUPS
CHUNKS = 5
SENT = TILE + 8
LOG2E = 1.4426950408889634
LARGE = pltpu.CompilerParams(vmem_limit_bytes=44 * 1024 * 1024)
FIRST = pltpu.CompilerParams(vmem_limit_bytes=(64 * 1024 - 64) * 1024)
OUTPUTS = pltpu.CompilerParams(vmem_limit_bytes=58 * 1024 * 1024)
STACK = pltpu.CompilerParams(vmem_limit_bytes=24 * 1024 * 1024)
SMALL = pltpu.CompilerParams(vmem_limit_bytes=16 * 1024 * 1024)

STORE_GROUPS = [
    [(p * 4 + (turn + t) % 4) * 4 + t for p in range(PROMPTS) for t in range(LANES)]
    for turn in range(4)
]
PICK_GROUPS = [
    [z * 32 + x * 8 + high * 4 + block for x in range(4) for block in range(4)]
    for z in range(2)
    for high in range(2)
]


def over_store(array):
    return lax.all_to_all(
        array,
        ("resp", "tp"),
        split_axis=0,
        concat_axis=0,
        tiled=True,
        axis_index_groups=STORE_GROUPS,
    )


def over_pick(array):
    return lax.all_to_all(
        array, "resp", split_axis=0, concat_axis=0, tiled=True, axis_index_groups=PICK_GROUPS
    )


def column_of(x):
    return (x // KV_LANE, x % KV_LANE)


def stored_kernel(
    owner_hbm, key_hbm, value_hbm, out_ref, owner_ref, key_ref, value_ref, sems
):
    copies = [
        pltpu.make_async_copy(source, target, sems.at[at])
        for at, (source, target) in enumerate(
            ((owner_hbm, owner_ref), (key_hbm, key_ref), (value_hbm, value_ref))
        )
    ]
    for copy in copies:
        copy.start()
    for copy in copies:
        copy.wait()
    at = lax.broadcasted_iota(jnp.int32, (SENT - TILE, HD), 1)
    asked = jnp.zeros((SENT - TILE, HD), jnp.int32)
    for one in range(LOCAL):
        asked = jnp.where(at == one, owner_ref[one], asked)
    asked = asked.astype(jnp.float32).astype(jnp.bfloat16)
    for prompt in range(PROMPTS):
        which, head = column_of(prompt // 2 % 4)
        source = value_ref if which else key_ref
        for lane in range(LANES):
            first = (lane * KV_LANE + head) * HD
            out_ref[prompt * LANES + lane] = jnp.concatenate(
                [source[:, first : first + HD], asked], 0
            )


def pick_kernel(pieces_ref, out_ref, owner_ref, owners, sem):
    resp = lax.axis_index("resp")
    prompt = resp // 4
    turn = (resp % 4 + LANES - lax.axis_index("tp")) % 4
    for x in range(4):
        for block in range(4):
            source = (prompt // 8 * 8 + x * 2 + prompt % 2) * LANES + (block + 4 - turn) % 4
            tile = pieces_ref[source].astype(jnp.float32)
            owner_ref[x * 4 + block : x * 4 + block + 1] = tile[TILE : TILE + 1].astype(jnp.int32)
    copy = pltpu.make_async_copy(owner_ref, owners, sem)
    copy.start()
    copy.wait()
    for member in range(MEMBERS):
        for one in range(LOCAL):
            owner = owners[member, one]
            for lane in range(LANES):
                out_ref[member, one, lane * TILE : (lane + 1) * TILE] = pieces_ref[
                    owner * LANES + lane, :TILE
                ]


def fold_kernel(owner_ref, terms_ref, token_ref, out_ref, total):
    total[...] = jnp.zeros_like(total)
    for one in range(LOCAL):
        for member in range(MEMBERS):
            owner = owner_ref[member, one]
            total[owner] += terms_ref[member, one].astype(jnp.float32)
    for prompt in range(PROMPTS):
        for lane in range(LANES):
            out_ref[prompt * LANES + lane] = total[
                prompt, lane * TILE : (lane + 1) * TILE
            ].astype(out_ref.dtype)


def summed_kernel(sums_ref, key_ref, value_ref):
    for x in range(4):
        which, head = column_of(x)
        target = value_ref if which else key_ref
        for lane in range(LANES):
            tile = jnp.zeros((TILE, HD), jnp.float32)
            for z in range(2):
                for high in range(2):
                    source = (z * 8 + x * 2 + high) * LANES + lane
                    tile = tile + sums_ref[source].astype(jnp.float32)
            first = (lane * KV_LANE + head) * HD
            target[:, first : first + HD] = tile.astype(target.dtype)


def heads(head):
    for at in range(PER_GROUP):
        column = (head * PER_GROUP + at) * HD
        yield slice(at * ROWS, (at + 1) * ROWS), slice(column, column + HD)


def by_length(length, span, work, blank):
    for first in range(0, span, 2 * ROWS):
        second = first + ROWS
        last = min(second + ROWS, span)
        if second < span:

            @pl.when(length > second)
            def _():
                work((first, second))

        @pl.when((length > first) & ((length <= second) | (second >= span)))
        def _():
            work((first,))
            if second < span:
                blank(second, last)

        @pl.when(length <= first)
        def _():
            blank(first, last)


def kept_copies(kept, held, sems, response, head, first, out):
    chunk = first // ROWS
    rows = pl.ds(0, LP + first + ROWS)
    for at in range(2):
        far = kept[at].at[response, head, chunk, rows]
        near = held[at].at[response, head, chunk, rows]
        source, target = (near, far) if out else (far, near)
        yield pltpu.make_async_copy(source, target, sems.at[response, head, chunk, at])


def each_live(length_ref, span, act):
    for response in range(LOCAL):
        for first in range(0, span, ROWS):

            @pl.when(length_ref[response] > first)
            def _():
                for head in range(KV_LANE):
                    act(response, head, first)


def stack_kernel(query_ref, grad_ref, stacked_query, stacked_grad):
    response = pl.program_id(0)
    for chunk in range(CHUNKS):
        rows = slice(chunk * ROWS, (chunk + 1) * ROWS)
        for head in range(KV_LANE):
            for part, column in heads(head):
                stacked_query[response, head, chunk, part] = query_ref[rows, column]
                stacked_grad[response, head, chunk, part] = grad_ref[rows, column]


def attend_kernel(
    length_ref,
    stacked_query,
    stacked_grad,
    key_ref,
    value_ref,
    prompt_ref,
    key_grad_ref,
    value_grad_ref,
    prompt_grad_ref,
    probability_hbm,
    score_grad_hbm,
    keys,
    values,
    scores,
    prob_grads,
    probability_ref,
    score_grad_ref,
    key_total,
    value_total,
    sems,
):
    kept = (probability_hbm, score_grad_hbm)
    held = (probability_ref, score_grad_ref)
    response = pl.program_id(0)
    length = length_ref[response]
    span = key_ref.shape[0]
    scale = HD**-0.5
    wide = PER_GROUP * ROWS
    for head in range(KV_LANE):
        for whole, own_ref, which in ((keys, key_ref, 0), (values, value_ref, 1)):
            whole[head, :LP] = prompt_ref[which, head, :, 0].reshape(LP, HD)
            whole[head, LP:] = own_ref[:, head * HD : (head + 1) * HD]

    def score(slot, head, first):
        count = LP + first + ROWS
        lane = lax.broadcasted_iota(jnp.int32, (1, wide), 1) % ROWS
        causal = lax.broadcasted_iota(jnp.int32, (ROWS, 1), 0) <= lane
        raw = lax.dot_general(
            keys[head, :count],
            stacked_query[response, head, first // ROWS],
            (((1,), (1,)), ((), ())),
            preferred_element_type=jnp.float32,
        )
        tail = jnp.where(causal, raw[count - ROWS :], -1e30)
        scores[slot, : count - ROWS] = raw[: count - ROWS]
        scores[slot, count - ROWS : count] = tail
        top = jnp.max(raw[: count - ROWS].reshape(-1, 8, wide), axis=0)
        top = jnp.maximum(top, jnp.max(tail.reshape(-1, 8, wide), axis=0))
        prob_grads[slot, :count] = lax.dot_general(
            values[head, :count],
            stacked_grad[response, head, first // ROWS],
            (((1,), (1,)), ((), ())),
            preferred_element_type=jnp.float32,
        )
        return jnp.max(top, axis=0, keepdims=True) * (scale * LOG2E)

    def soften(slot, head, first, largest):
        count = LP + first + ROWS
        chunk = first // ROWS
        lane = lax.broadcasted_iota(jnp.int32, (1, wide), 1) % ROWS
        live = first + lane < length
        blocks = [slice(at, at + ROWS) for at in range(0, count, ROWS)]
        total = jnp.zeros((8, wide), jnp.float32)
        moved = jnp.zeros((8, wide), jnp.float32)
        for block in blocks:
            weights = jnp.exp2(scores[slot, block] * (scale * LOG2E) - largest)
            scores[slot, block] = weights
            total = total + jnp.sum(weights.reshape(-1, 8, wide), axis=0)
            terms = weights * prob_grads[slot, block]
            moved = moved + jnp.sum(terms.reshape(-1, 8, wide), axis=0)
        inverse = jnp.where(live, 1.0 / jnp.sum(total, axis=0, keepdims=True), 0.0)
        delta = jnp.sum(moved, axis=0, keepdims=True) * inverse
        for block in blocks:
            probability = scores[slot, block] * inverse
            probability_ref[response, head, chunk, block] = probability.astype(jnp.bfloat16)
            score_grad_ref[response, head, chunk, block] = (
                probability * (prob_grads[slot, block] - delta)
            ).astype(jnp.bfloat16)

    def gather(slot, head, first):
        count = LP + first + ROWS
        chunk = first // ROWS
        for total, left_ref, stacked in (
            (value_total, probability_ref, stacked_grad),
            (key_total, score_grad_ref, stacked_query),
        ):
            terms = jnp.dot(
                left_ref[response, head, chunk, :count],
                stacked[response, head, chunk],
                preferred_element_type=jnp.float32,
            )
            if first == 0:
                total[head, :count] = terms
            else:
                total[head, : count - ROWS] += terms[: count - ROWS]
                total[head, count - ROWS : count] = terms[count - ROWS :]

    def work(firsts):
        streams = [(head, first) for first in firsts for head in range(KV_LANE)]
        largest = {0: score(0, *streams[0])}
        for slot, stream in enumerate(streams):
            if slot + 1 < len(streams):
                largest[slot + 1] = score(slot + 1, *streams[slot + 1])
            soften(slot, *stream, largest[slot])
            for copy in kept_copies(kept, held, sems, response, *stream, True):
                copy.start()
            gather(slot, *stream)

    def blank(first, last):
        zeros = jnp.zeros((KV_LANE, last - first, HD), jnp.float32)
        key_total[:, LP + first : LP + last] = zeros
        value_total[:, LP + first : LP + last] = zeros

    by_length(length, span, work, blank)

    for head in range(KV_LANE):
        lanes = slice(head * HD, (head + 1) * HD)
        key_terms = (key_total[head] * scale).astype(jnp.bfloat16)
        value_terms = value_total[head].astype(jnp.bfloat16)
        prompt_grad_ref[0, head, :, 0] = key_terms[:LP].reshape(GROUPS, SLICE, HD)
        prompt_grad_ref[1, head, :, 0] = value_terms[:LP].reshape(GROUPS, SLICE, HD)
        key_grad_ref[:, lanes] = key_terms[LP:]
        value_grad_ref[:, lanes] = value_terms[LP:]

    def finish(*chunk):
        for copy in kept_copies(kept, held, sems, *chunk, True):
            copy.wait()

    @pl.when(response == LOCAL - 1)
    def _():
        each_live(length_ref, span, finish)


def outputs_kernel(
    length_ref,
    key_ref,
    value_ref,
    prompt_ref,
    probability_hbm,
    score_grad_hbm,
    out_ref,
    query_grad_ref,
    token_ref,
    keys_t,
    values_t,
    probability_ref,
    score_grad_ref,
    sems,
):
    kept = (probability_hbm, score_grad_hbm)
    held = (probability_ref, score_grad_ref)
    response = pl.program_id(0)
    length = length_ref[response]
    span = out_ref.shape[0]
    scale = HD**-0.5

    def fetch(*chunk):
        for copy in kept_copies(kept, held, sems, *chunk, False):
            copy.start()

    @pl.when(response == 0)
    def _():
        each_live(length_ref, span, fetch)

    for head in range(KV_LANE):
        lanes = slice(head * HD, (head + 1) * HD)
        for whole_t, own_ref, which in ((keys_t, key_ref, 0), (values_t, value_ref, 1)):
            whole_t[head] = jnp.concatenate(
                [prompt_ref[which, head, :, 0].reshape(LP, HD), own_ref[:, lanes]], 0
            ).T

    def work(firsts):
        for first in firsts:
            count = LP + first + ROWS
            chunk = first // ROWS
            rows = slice(first, first + ROWS)
            for head in range(KV_LANE):
                for copy in kept_copies(kept, held, sems, response, head, first, False):
                    copy.wait()
            for head in range(KV_LANE):
                output = jnp.dot(
                    values_t[head, :, :count],
                    probability_ref[response, head, chunk, :count],
                    preferred_element_type=jnp.float32,
                )
                query_grad = jnp.dot(
                    keys_t[head, :, :count],
                    score_grad_ref[response, head, chunk, :count],
                    preferred_element_type=jnp.float32,
                )
                output = output.astype(jnp.bfloat16).T
                query_grad = (query_grad * scale).astype(jnp.bfloat16).T
                for part, column in heads(head):
                    out_ref[rows, column] = output[part]
                    query_grad_ref[rows, column] = query_grad[part]

    def blank(first, last):
        zeros = jnp.zeros((last - first, out_ref.shape[1]), jnp.bfloat16)
        out_ref[first:last, :] = zeros
        query_grad_ref[first:last, :] = zeros

    by_length(length, span, work, blank)
    token_ref[...] = jnp.zeros_like(token_ref)


def specs(span, wide, narrow):
    return dict(
        wide=pl.BlockSpec((span, wide), lambda i, length: (i, 0)),
        narrow=pl.BlockSpec((span, narrow), lambda i, length: (i, 0)),
        prompt=pl.BlockSpec(
            (2, KV_LANE, GROUPS, 1, SLICE, HD), lambda i, length: (0, 0, 0, i, 0, 0)
        ),
        held=pl.BlockSpec(memory_space=pltpu.VMEM),
        kept=pl.BlockSpec(memory_space=pl.ANY),
    )


def stack(queries, out_grad, count):
    span = queries.shape[0] // count
    shape = jax.ShapeDtypeStruct(
        (count, KV_LANE, CHUNKS, PER_GROUP * ROWS, HD), jnp.bfloat16
    )
    wide = pl.BlockSpec((span, queries.shape[1]), lambda i: (i, 0))
    return pl.pallas_call(
        stack_kernel,
        out_shape=(shape, shape),
        grid=(count,),
        in_specs=[wide, wide],
        out_specs=[pl.BlockSpec(memory_space=pltpu.VMEM)] * 2,
        compiler_params=STACK,
        cost_estimate=pl.CostEstimate(
            flops=0, bytes_accessed=8 * queries.size, transcendentals=0
        ),
    )(queries, out_grad)


def attend(lengths, stacked_query, stacked_grad, resp_keys, resp_values, prompt_rows):
    count = lengths.shape[0]
    span = resp_keys.shape[0] // count
    both = LP + span
    streams = 2 * KV_LANE
    stacked = PER_GROUP * ROWS
    elements = stacked_query.size
    spec = specs(span, stacked_query.size // resp_keys.shape[0], resp_keys.shape[1])
    kept = jax.ShapeDtypeStruct((count, KV_LANE, CHUNKS, both, stacked), jnp.bfloat16)
    return pl.pallas_call(
        attend_kernel,
        out_shape=(
            jax.ShapeDtypeStruct(resp_keys.shape, jnp.bfloat16),
            jax.ShapeDtypeStruct(resp_keys.shape, jnp.bfloat16),
            jax.ShapeDtypeStruct(prompt_rows.shape, jnp.bfloat16),
            kept,
            kept,
        ),
        grid_spec=pltpu.PrefetchScalarGridSpec(
            num_scalar_prefetch=1,
            grid=(count,),
            in_specs=[spec[name] for name in ("held", "held", "narrow", "narrow", "prompt")],
            out_specs=[spec[name] for name in ("narrow", "narrow", "prompt", "kept", "kept")],
            scratch_shapes=[
                pltpu.VMEM((KV_LANE, both, HD), jnp.bfloat16),
                pltpu.VMEM((KV_LANE, both, HD), jnp.bfloat16),
                pltpu.VMEM((streams, both, stacked), jnp.float32),
                pltpu.VMEM((streams, both, stacked), jnp.float32),
                pltpu.VMEM(kept.shape, jnp.bfloat16),
                pltpu.VMEM(kept.shape, jnp.bfloat16),
                pltpu.VMEM((KV_LANE, both, HD), jnp.float32),
                pltpu.VMEM((KV_LANE, both, HD), jnp.float32),
                pltpu.SemaphoreType.DMA((LOCAL, KV_LANE, CHUNKS, 2)),
            ],
        ),
        compiler_params=LARGE,
        cost_estimate=pl.CostEstimate(
            flops=16 * elements * both,
            bytes_accessed=4 * elements,
            transcendentals=elements * both // HD,
        ),
    )(lengths, stacked_query, stacked_grad, resp_keys, resp_values, prompt_rows)


def outputs(lengths, resp_keys, resp_values, prompt_rows, probability, score_grad, wide):
    count = lengths.shape[0]
    rows = resp_keys.shape[0]
    span = rows // count
    both = LP + span
    spec = specs(span, wide, resp_keys.shape[1])
    shape = jax.ShapeDtypeStruct((rows, wide), jnp.bfloat16)
    return pl.pallas_call(
        outputs_kernel,
        out_shape=(shape, shape, jax.ShapeDtypeStruct((8, HD), jnp.int32)),
        grid_spec=pltpu.PrefetchScalarGridSpec(
            num_scalar_prefetch=1,
            grid=(count,),
            in_specs=[spec[name] for name in ("narrow", "narrow", "prompt", "kept", "kept")],
            out_specs=[
                spec["wide"],
                spec["wide"],
                pl.BlockSpec((8, HD), lambda i, length: (0, 0)),
            ],
            scratch_shapes=[
                pltpu.VMEM((KV_LANE, HD, both), jnp.bfloat16),
                pltpu.VMEM((KV_LANE, HD, both), jnp.bfloat16),
                pltpu.VMEM(probability.shape, jnp.bfloat16),
                pltpu.VMEM(score_grad.shape, jnp.bfloat16),
                pltpu.SemaphoreType.DMA((LOCAL, KV_LANE, CHUNKS, 2)),
            ],
        ),
        compiler_params=OUTPUTS,
        cost_estimate=pl.CostEstimate(
            flops=8 * rows * wide * both,
            bytes_accessed=4 * rows * wide + 4 * probability.size,
            transcendentals=0,
        ),
    )(lengths, resp_keys, resp_values, prompt_rows, probability, score_grad)


def whole(kernel, out_shape, spaces, *operands, params=SMALL, **more):
    return pl.pallas_call(
        kernel,
        out_shape=out_shape,
        in_specs=[pl.BlockSpec(memory_space=space) for space in spaces],
        compiler_params=params,
        **more,
    )(*operands)


def low(*shape):
    return jax.ShapeDtypeStruct(shape, jnp.bfloat16)


def shards(
    queries, resp_keys, resp_values, out_grad, prompt_keys, prompt_values, lengths, prompt_of
):
    pieces = over_store(
        whole(
            stored_kernel,
            low(PROMPTS * LANES, SENT, HD),
            [pltpu.HBM] * 3,
            prompt_of,
            prompt_keys,
            prompt_values,
            params=FIRST,
            scratch_shapes=[
                pltpu.SMEM(prompt_of.shape, jnp.int32),
                pltpu.VMEM(prompt_keys.shape, jnp.bfloat16),
                pltpu.VMEM(prompt_values.shape, jnp.bfloat16),
                pltpu.SemaphoreType.DMA((3,)),
            ],
        )
    )
    picked, owners = whole(
        pick_kernel,
        (low(MEMBERS, LOCAL, SLICE, HD), jax.ShapeDtypeStruct((MEMBERS, HD), jnp.int32)),
        [pltpu.VMEM],
        pieces,
        scratch_shapes=[pltpu.SMEM((MEMBERS, HD), jnp.int32), pltpu.SemaphoreType.DMA],
    )
    prompt_rows = over_pick(picked).reshape(2, KV_LANE, GROUPS, LOCAL, SLICE, HD)
    stacked = stack(queries, out_grad, lengths.shape[0])
    resp_key_grad, resp_value_grad, terms, probability, score_grad = attend(
        lengths, *stacked, resp_keys, resp_values, prompt_rows
    )
    terms = over_pick(terms.reshape(MEMBERS, LOCAL, SLICE, HD))
    attn_out, query_grad, token = outputs(
        lengths, resp_keys, resp_values, prompt_rows, probability, score_grad, queries.shape[1]
    )
    sums = whole(
        fold_kernel,
        low(PROMPTS * LANES, TILE, HD),
        [pltpu.SMEM, pltpu.VMEM, pl.ANY],
        owners,
        terms,
        token,
        scratch_shapes=[pltpu.VMEM((PROMPTS, SLICE, HD), jnp.float32)],
    )
    prompt_key_grad, prompt_value_grad = whole(
        summed_kernel,
        (low(*prompt_keys.shape), low(*prompt_values.shape)),
        [pltpu.VMEM],
        over_store(sums),
    )
    return (
        attn_out,
        query_grad,
        resp_key_grad,
        resp_value_grad,
        prompt_key_grad,
        prompt_value_grad,
    )


def solution(mesh):
    wide = P("resp", "tp")
    stored = P(("resp", "tp"), None)
    return jax.shard_map(
        shards,
        mesh=mesh,
        in_specs=(wide, wide, wide, wide, stored, stored, P("resp"), P("resp")),
        out_specs=(wide, wide, wide, wide, stored, stored),
        check_vma=False,
    )
```

```python
import functools

import jax
import jax.numpy as jnp
from jax import lax
from jax.experimental import pallas as pl
from jax.experimental.pallas import tpu as pltpu
from jax.sharding import PartitionSpec as P

HD = 128
LP = 256
ROWS = 32
PER_GROUP = 8
KV_LANE = 2
LANES = 4
GROUPS = 4
TILE = 16
MEMBERS = 16
PROMPTS = 16
LOCAL = 4
SLICE = LP // GROUPS
CHUNKS = 5
HALF = LOCAL // 2
SENT = TILE + 8
LOG2E = 1.4426950408889634
LARGE = pltpu.CompilerParams(vmem_limit_bytes=48 * 1024 * 1024)
FIRST = pltpu.CompilerParams(vmem_limit_bytes=(64 * 1024 - 64) * 1024)
SMALL = pltpu.CompilerParams(vmem_limit_bytes=16 * 1024 * 1024)

STORE_GROUPS = [
    [(p * 4 + (turn + t) % 4) * 4 + t for p in range(PROMPTS) for t in range(LANES)]
    for turn in range(4)
]
PICK_GROUPS = [
    [z * 32 + x * 8 + high * 4 + block for x in range(4) for block in range(4)]
    for z in range(2)
    for high in range(2)
]


def over_store(array):
    return lax.all_to_all(
        array,
        ("resp", "tp"),
        split_axis=0,
        concat_axis=0,
        tiled=True,
        axis_index_groups=STORE_GROUPS,
    )


def over_pick(array):
    return lax.all_to_all(
        array, "resp", split_axis=0, concat_axis=0, tiled=True, axis_index_groups=PICK_GROUPS
    )


def column_of(x):
    return (x // KV_LANE, x % KV_LANE)


def stored_kernel(
    owner_hbm, key_hbm, value_hbm, out_ref, owner_ref, key_ref, value_ref, sems
):
    copies = [
        pltpu.make_async_copy(source, target, sems.at[at])
        for at, (source, target) in enumerate(
            ((owner_hbm, owner_ref), (key_hbm, key_ref), (value_hbm, value_ref))
        )
    ]
    for copy in copies:
        copy.start()
    for copy in copies:
        copy.wait()
    at = lax.broadcasted_iota(jnp.int32, (SENT - TILE, HD), 1)
    asked = jnp.zeros((SENT - TILE, HD), jnp.int32)
    for one in range(LOCAL):
        asked = jnp.where(at == one, owner_ref[one], asked)
    asked = asked.astype(jnp.float32).astype(jnp.bfloat16)
    for prompt in range(PROMPTS):
        which, head = column_of(prompt // 2 % 4)
        source = value_ref if which else key_ref
        for lane in range(LANES):
            first = (lane * KV_LANE + head) * HD
            out_ref[prompt * LANES + lane] = jnp.concatenate(
                [source[:, first : first + HD], asked], 0
            )


def pick_kernel(pieces_ref, out_ref, owner_ref, owners, sem):
    resp = lax.axis_index("resp")
    prompt = resp // 4
    turn = (resp % 4 + LANES - lax.axis_index("tp")) % 4
    for x in range(4):
        for block in range(4):
            source = (prompt // 8 * 8 + x * 2 + prompt % 2) * LANES + (block + 4 - turn) % 4
            tile = pieces_ref[source].astype(jnp.float32)
            owner_ref[x * 4 + block : x * 4 + block + 1] = tile[TILE : TILE + 1].astype(jnp.int32)
    copy = pltpu.make_async_copy(owner_ref, owners, sem)
    copy.start()
    copy.wait()
    for member in range(MEMBERS):
        for one in range(LOCAL):
            owner = owners[member, one]
            for lane in range(LANES):
                out_ref[member, one, lane * TILE : (lane + 1) * TILE] = pieces_ref[
                    owner * LANES + lane, :TILE
                ]


def fold_kernel(owner_ref, terms_ref, token_ref, out_ref, total):
    total[...] = jnp.zeros_like(total)
    for one in range(LOCAL):
        for member in range(MEMBERS):
            owner = owner_ref[member, one]
            total[owner] += terms_ref[member, one].astype(jnp.float32)
    for prompt in range(PROMPTS):
        for lane in range(LANES):
            out_ref[prompt * LANES + lane] = total[
                prompt, lane * TILE : (lane + 1) * TILE
            ].astype(out_ref.dtype)


def summed_kernel(sums_ref, token_ref, key_ref, value_ref):
    for x in range(4):
        which, head = column_of(x)
        target = value_ref if which else key_ref
        for lane in range(LANES):
            tile = jnp.zeros((TILE, HD), jnp.float32)
            for z in range(2):
                for high in range(2):
                    source = (z * 8 + x * 2 + high) * LANES + lane
                    tile = tile + sums_ref[source].astype(jnp.float32)
            first = (lane * KV_LANE + head) * HD
            target[:, first : first + HD] = tile.astype(target.dtype)


def heads(head):
    for at in range(PER_GROUP):
        column = (head * PER_GROUP + at) * HD
        yield slice(at * ROWS, (at + 1) * ROWS), slice(column, column + HD)


def by_length(length, span, work, blank):
    for first in range(0, span, 2 * ROWS):
        second = first + ROWS
        last = min(second + ROWS, span)
        if second < span:

            @pl.when(length > second)
            def _():
                work((first, second))

        @pl.when((length > first) & ((length <= second) | (second >= span)))
        def _():
            work((first,))
            if second < span:
                blank(second, last)

        @pl.when(length <= first)
        def _():
            blank(first, last)


def kept_copies(kept, held, sems, response, slot, head, first, out):
    chunk = first // ROWS
    rows = pl.ds(0, LP + first + ROWS)
    for at in range(2):
        far = kept.at[response, at, head, chunk, rows]
        near = held[at].at[slot, head, chunk, rows]
        source, target = (near, far) if out else (far, near)
        yield pltpu.make_async_copy(source, target, sems.at[slot, head, chunk, at])


def each_live(length_ref, start, count, span, act):
    for slot in range(count):
        for first in range(0, span, ROWS):

            @pl.when(length_ref[start + slot] > first)
            def _():
                for head in range(KV_LANE):
                    act(start + slot, slot, head, first)


def attend_kernel(
    length_ref,
    query_ref,
    grad_ref,
    key_ref,
    value_ref,
    prompt_ref,
    key_grad_ref,
    value_grad_ref,
    prompt_grad_ref,
    kept,
    keys,
    values,
    stacked_query,
    stacked_grad,
    scores,
    prob_grads,
    probability_ref,
    score_grad_ref,
    key_total,
    value_total,
    sems,
):
    held = (probability_ref, score_grad_ref)
    response = pl.program_id(0)
    length = length_ref[response]
    span = key_ref.shape[0]
    scale = HD**-0.5
    wide = PER_GROUP * ROWS
    for head in range(KV_LANE):
        for whole, own_ref, which in ((keys, key_ref, 0), (values, value_ref, 1)):
            whole[head, :LP] = prompt_ref[which, head, :, 0].reshape(LP, HD)
            whole[head, LP:] = own_ref[:, head * HD : (head + 1) * HD]

    def score(slot, head, first):
        count = LP + first + ROWS
        lane = lax.broadcasted_iota(jnp.int32, (1, wide), 1) % ROWS
        causal = lax.broadcasted_iota(jnp.int32, (ROWS, 1), 0) <= lane
        for part, column in heads(head):
            stacked_query[slot, part] = query_ref[first : first + ROWS, column]
            stacked_grad[slot, part] = grad_ref[first : first + ROWS, column]
        raw = lax.dot_general(
            keys[head, :count],
            stacked_query[slot],
            (((1,), (1,)), ((), ())),
            preferred_element_type=jnp.float32,
        )
        tail = jnp.where(causal, raw[count - ROWS :], -1e30)
        scores[slot, : count - ROWS] = raw[: count - ROWS]
        scores[slot, count - ROWS : count] = tail
        top = jnp.max(raw[: count - ROWS].reshape(-1, 8, wide), axis=0)
        top = jnp.maximum(top, jnp.max(tail.reshape(-1, 8, wide), axis=0))
        prob_grads[slot, :count] = lax.dot_general(
            values[head, :count],
            stacked_grad[slot],
            (((1,), (1,)), ((), ())),
            preferred_element_type=jnp.float32,
        )
        return jnp.max(top, axis=0, keepdims=True) * (scale * LOG2E)

    def soften(slot, head, first, largest):
        count = LP + first + ROWS
        chunk = first // ROWS
        lane = lax.broadcasted_iota(jnp.int32, (1, wide), 1) % ROWS
        live = first + lane < length
        blocks = [slice(at, at + ROWS) for at in range(0, count, ROWS)]
        total = jnp.zeros((8, wide), jnp.float32)
        moved = jnp.zeros((8, wide), jnp.float32)
        for block in blocks:
            weights = jnp.exp2(scores[slot, block] * (scale * LOG2E) - largest)
            scores[slot, block] = weights
            total = total + jnp.sum(weights.reshape(-1, 8, wide), axis=0)
            terms = weights * prob_grads[slot, block]
            moved = moved + jnp.sum(terms.reshape(-1, 8, wide), axis=0)
        inverse = jnp.where(live, 1.0 / jnp.sum(total, axis=0, keepdims=True), 0.0)
        delta = jnp.sum(moved, axis=0, keepdims=True) * inverse
        for block in blocks:
            probability = scores[slot, block] * inverse
            probability_ref[response, head, chunk, block] = probability.astype(jnp.bfloat16)
            score_grad_ref[response, head, chunk, block] = (
                probability * (prob_grads[slot, block] - delta)
            ).astype(jnp.bfloat16)

    def gather(slot, head, first):
        count = LP + first + ROWS
        chunk = first // ROWS
        for total, left_ref, stacked in (
            (value_total, probability_ref, stacked_grad),
            (key_total, score_grad_ref, stacked_query),
        ):
            terms = jnp.dot(
                left_ref[response, head, chunk, :count],
                stacked[slot],
                preferred_element_type=jnp.float32,
            )
            if first == 0:
                total[head, :count] = terms
            else:
                total[head, : count - ROWS] += terms[: count - ROWS]
                total[head, count - ROWS : count] = terms[count - ROWS :]

    def work(firsts):
        streams = [(head, first) for first in firsts for head in range(KV_LANE)]
        largest = {0: score(0, *streams[0])}
        for slot, stream in enumerate(streams):
            if slot + 1 < len(streams):
                largest[slot + 1] = score(slot + 1, *streams[slot + 1])
            soften(slot, *stream, largest[slot])
            for copy in kept_copies(kept, held, sems, response, response, *stream, True):
                copy.start()
            gather(slot, *stream)

    def blank(first, last):
        zeros = jnp.zeros((KV_LANE, last - first, HD), jnp.float32)
        key_total[:, LP + first : LP + last] = zeros
        value_total[:, LP + first : LP + last] = zeros

    by_length(length, span, work, blank)

    for head in range(KV_LANE):
        lanes = slice(head * HD, (head + 1) * HD)
        key_terms = (key_total[head] * scale).astype(jnp.bfloat16)
        value_terms = value_total[head].astype(jnp.bfloat16)
        prompt_grad_ref[0, head, :, 0] = key_terms[:LP].reshape(GROUPS, SLICE, HD)
        prompt_grad_ref[1, head, :, 0] = value_terms[:LP].reshape(GROUPS, SLICE, HD)
        key_grad_ref[:, lanes] = key_terms[LP:]
        value_grad_ref[:, lanes] = value_terms[LP:]

    def finish(*chunk):
        for copy in kept_copies(kept, held, sems, *chunk, True):
            copy.wait()

    @pl.when(response == LOCAL - 1)
    def _():
        each_live(length_ref, 0, LOCAL, span, finish)


def outputs_kernel(start, length_ref, key_ref, value_ref, prompt_ref, kept, *rest):
    out_ref, query_grad_ref, token_ref, *rest = rest[-8:]
    keys_t, values_t, probability_ref, score_grad_ref, sems = rest
    held = (probability_ref, score_grad_ref)
    slot = pl.program_id(0)
    response = start + slot
    length = length_ref[response]
    span = out_ref.shape[0]
    scale = HD**-0.5

    def fetch(*chunk):
        for copy in kept_copies(kept, held, sems, *chunk, False):
            copy.start()

    @pl.when(slot == 0)
    def _():
        each_live(length_ref, start, HALF, span, fetch)

    for head in range(KV_LANE):
        lanes = slice(head * HD, (head + 1) * HD)
        for whole_t, own_ref, which in ((keys_t, key_ref, 0), (values_t, value_ref, 1)):
            whole_t[head] = jnp.concatenate(
                [prompt_ref[which, head, :, 0].reshape(LP, HD), own_ref[:, lanes]], 0
            ).T

    def work(firsts):
        for first in firsts:
            count = LP + first + ROWS
            chunk = first // ROWS
            rows = slice(first, first + ROWS)
            for head in range(KV_LANE):
                for copy in kept_copies(kept, held, sems, response, slot, head, first, False):
                    copy.wait()
            for head in range(KV_LANE):
                output = jnp.dot(
                    values_t[head, :, :count],
                    probability_ref[slot, head, chunk, :count],
                    preferred_element_type=jnp.float32,
                )
                query_grad = jnp.dot(
                    keys_t[head, :, :count],
                    score_grad_ref[slot, head, chunk, :count],
                    preferred_element_type=jnp.float32,
                )
                output = output.astype(jnp.bfloat16).T
                query_grad = (query_grad * scale).astype(jnp.bfloat16).T
                for part, column in heads(head):
                    out_ref[rows, column] = output[part]
                    query_grad_ref[rows, column] = query_grad[part]

    def blank(first, last):
        zeros = jnp.zeros((last - first, out_ref.shape[1]), jnp.bfloat16)
        out_ref[first:last, :] = zeros
        query_grad_ref[first:last, :] = zeros

    by_length(length, span, work, blank)
    token_ref[...] = jnp.zeros_like(token_ref)


def specs(span, wide, narrow, start=0):
    return dict(
        wide=pl.BlockSpec((span, wide), lambda i, length: (start + i, 0)),
        narrow=pl.BlockSpec((span, narrow), lambda i, length: (start + i, 0)),
        prompt=pl.BlockSpec(
            (2, KV_LANE, GROUPS, 1, SLICE, HD), lambda i, length: (0, 0, 0, start + i, 0, 0)
        ),
        kept=pl.BlockSpec(memory_space=pl.ANY),
    )


def attend(lengths, queries, out_grad, resp_keys, resp_values, prompt_rows):
    count = lengths.shape[0]
    span = queries.shape[0] // count
    both = LP + span
    streams = 2 * KV_LANE
    stacked = PER_GROUP * ROWS
    spec = specs(span, queries.shape[1], resp_keys.shape[1])
    held = (count, KV_LANE, CHUNKS, both, stacked)
    return pl.pallas_call(
        attend_kernel,
        out_shape=(
            jax.ShapeDtypeStruct(resp_keys.shape, jnp.bfloat16),
            jax.ShapeDtypeStruct(resp_keys.shape, jnp.bfloat16),
            jax.ShapeDtypeStruct(prompt_rows.shape, jnp.bfloat16),
            jax.ShapeDtypeStruct((count, 2, KV_LANE, CHUNKS, both, stacked), jnp.bfloat16),
        ),
        grid_spec=pltpu.PrefetchScalarGridSpec(
            num_scalar_prefetch=1,
            grid=(count,),
            in_specs=[spec[name] for name in ("wide", "wide", "narrow", "narrow", "prompt")],
            out_specs=[spec[name] for name in ("narrow", "narrow", "prompt", "kept")],
            scratch_shapes=[
                pltpu.VMEM((KV_LANE, both, HD), jnp.bfloat16),
                pltpu.VMEM((KV_LANE, both, HD), jnp.bfloat16),
                pltpu.VMEM((streams, stacked, HD), jnp.bfloat16),
                pltpu.VMEM((streams, stacked, HD), jnp.bfloat16),
                pltpu.VMEM((streams, both, stacked), jnp.float32),
                pltpu.VMEM((streams, both, stacked), jnp.float32),
                pltpu.VMEM(held, jnp.bfloat16),
                pltpu.VMEM(held, jnp.bfloat16),
                pltpu.VMEM((KV_LANE, both, HD), jnp.float32),
                pltpu.VMEM((KV_LANE, both, HD), jnp.float32),
                pltpu.SemaphoreType.DMA((count, KV_LANE, CHUNKS, 2)),
            ],
        ),
        compiler_params=LARGE,
        cost_estimate=pl.CostEstimate(
            flops=16 * queries.size * both,
            bytes_accessed=4 * queries.size,
            transcendentals=queries.size * both // HD,
        ),
    )(lengths, queries, out_grad, resp_keys, resp_values, prompt_rows)


def outputs(lengths, resp_keys, resp_values, prompt_rows, kept, wide, start=0, earlier=()):
    rows = resp_keys.shape[0]
    span = rows // lengths.shape[0]
    both = LP + span
    spec = specs(span, wide, resp_keys.shape[1], start)
    held = (HALF, KV_LANE, CHUNKS, both, PER_GROUP * ROWS)
    shape = jax.ShapeDtypeStruct((rows, wide), jnp.bfloat16)
    return pl.pallas_call(
        functools.partial(outputs_kernel, start),
        out_shape=(shape, shape, jax.ShapeDtypeStruct((8, HD), jnp.int32)),
        grid_spec=pltpu.PrefetchScalarGridSpec(
            num_scalar_prefetch=1,
            grid=(HALF,),
            in_specs=[spec[name] for name in ("narrow", "narrow", "prompt", "kept")]
            + [spec["kept"]] * len(earlier),
            out_specs=[
                spec["wide"],
                spec["wide"],
                pl.BlockSpec((8, HD), lambda i, length: (0, 0)),
            ],
            scratch_shapes=[
                pltpu.VMEM((KV_LANE, HD, both), jnp.bfloat16),
                pltpu.VMEM((KV_LANE, HD, both), jnp.bfloat16),
                pltpu.VMEM(held, jnp.bfloat16),
                pltpu.VMEM(held, jnp.bfloat16),
                pltpu.SemaphoreType.DMA((HALF, KV_LANE, CHUNKS, 2)),
            ],
        ),
        input_output_aliases={5 + at: at for at in range(len(earlier[:2]))},
        compiler_params=LARGE,
        cost_estimate=pl.CostEstimate(
            flops=4 * rows * wide * both,
            bytes_accessed=2 * rows * wide + kept.size,
            transcendentals=0,
        ),
    )(lengths, resp_keys, resp_values, prompt_rows, kept, *earlier)


def whole(kernel, out_shape, spaces, *operands, params=SMALL, **more):
    return pl.pallas_call(
        kernel,
        out_shape=out_shape,
        in_specs=[pl.BlockSpec(memory_space=space) for space in spaces],
        compiler_params=params,
        **more,
    )(*operands)


def low(*shape):
    return jax.ShapeDtypeStruct(shape, jnp.bfloat16)


def shards(
    queries, resp_keys, resp_values, out_grad, prompt_keys, prompt_values, lengths, prompt_of
):
    pieces = over_store(
        whole(
            stored_kernel,
            low(PROMPTS * LANES, SENT, HD),
            [pltpu.HBM] * 3,
            prompt_of,
            prompt_keys,
            prompt_values,
            params=FIRST,
            scratch_shapes=[
                pltpu.SMEM(prompt_of.shape, jnp.int32),
                pltpu.VMEM(prompt_keys.shape, jnp.bfloat16),
                pltpu.VMEM(prompt_values.shape, jnp.bfloat16),
                pltpu.SemaphoreType.DMA((3,)),
            ],
        )
    )
    picked, owners = whole(
        pick_kernel,
        (low(MEMBERS, LOCAL, SLICE, HD), jax.ShapeDtypeStruct((MEMBERS, HD), jnp.int32)),
        [pltpu.VMEM],
        pieces,
        scratch_shapes=[pltpu.SMEM((MEMBERS, HD), jnp.int32), pltpu.SemaphoreType.DMA],
    )
    prompt_rows = over_pick(picked).reshape(2, KV_LANE, GROUPS, LOCAL, SLICE, HD)
    resp_key_grad, resp_value_grad, terms, kept = attend(
        lengths, queries, out_grad, resp_keys, resp_values, prompt_rows
    )
    terms = over_pick(terms.reshape(MEMBERS, LOCAL, SLICE, HD))
    shared = (lengths, resp_keys, resp_values, prompt_rows, kept, queries.shape[1])
    attn_out, query_grad, token = outputs(*shared)
    sums = whole(
        fold_kernel,
        low(PROMPTS * LANES, TILE, HD),
        [pltpu.SMEM, pltpu.VMEM, pl.ANY],
        owners,
        terms,
        token,
        scratch_shapes=[pltpu.VMEM((PROMPTS, SLICE, HD), jnp.float32)],
    )
    attn_out, query_grad, token = outputs(*shared, HALF, (attn_out, query_grad, sums))
    prompt_key_grad, prompt_value_grad = whole(
        summed_kernel,
        (low(*prompt_keys.shape), low(*prompt_values.shape)),
        [pltpu.VMEM, pl.ANY],
        over_store(sums),
        token,
    )
    return (
        attn_out,
        query_grad,
        resp_key_grad,
        resp_value_grad,
        prompt_key_grad,
        prompt_value_grad,
    )


def solution(mesh):
    wide = P("resp", "tp")
    stored = P(("resp", "tp"), None)
    return jax.shard_map(
        shards,
        mesh=mesh,
        in_specs=(wide, wide, wide, wide, stored, stored, P("resp"), P("resp")),
        out_specs=(wide, wide, wide, wide, stored, stored),
        check_vma=False,
    )
```

```python
import functools

import jax
import jax.numpy as jnp
from jax import lax
from jax.experimental import pallas as pl
from jax.experimental.pallas import tpu as pltpu
from jax.sharding import PartitionSpec as P

HD = 128
LP = 256
ROWS = 32
PER_GROUP = 8
KV_LANE = 2
LANES = 4
GROUPS = 4
TILE = 16
MEMBERS = 16
PROMPTS = 16
LOCAL = 4
SLICE = LP // GROUPS
CHUNKS = 5
HALF = LOCAL // 2
SENT = TILE + 8
LOG2E = 1.4426950408889634
LARGE = pltpu.CompilerParams(vmem_limit_bytes=48 * 1024 * 1024)
FIRST = pltpu.CompilerParams(vmem_limit_bytes=(64 * 1024 - 64) * 1024)
SMALL = pltpu.CompilerParams(vmem_limit_bytes=16 * 1024 * 1024)

STORE_GROUPS = [
    [(p * 4 + (turn + t) % 4) * 4 + t for p in range(PROMPTS) for t in range(LANES)]
    for turn in range(4)
]
PICK_GROUPS = [
    [z * 32 + x * 8 + high * 4 + block for x in range(4) for block in range(4)]
    for z in range(2)
    for high in range(2)
]


def over_store(array):
    return lax.all_to_all(
        array,
        ("resp", "tp"),
        split_axis=0,
        concat_axis=0,
        tiled=True,
        axis_index_groups=STORE_GROUPS,
    )


def over_pick(array):
    return lax.all_to_all(
        array, "resp", split_axis=0, concat_axis=0, tiled=True, axis_index_groups=PICK_GROUPS
    )


def column_of(x):
    return (x // KV_LANE, x % KV_LANE)


def stored_kernel(
    owner_hbm, key_hbm, value_hbm, out_ref, owner_ref, key_ref, value_ref, sems
):
    copies = [
        pltpu.make_async_copy(source, target, sems.at[at])
        for at, (source, target) in enumerate(
            ((owner_hbm, owner_ref), (key_hbm, key_ref), (value_hbm, value_ref))
        )
    ]
    for copy in copies:
        copy.start()
    for copy in copies:
        copy.wait()
    at = lax.broadcasted_iota(jnp.int32, (SENT - TILE, HD), 1)
    asked = jnp.zeros((SENT - TILE, HD), jnp.int32)
    for one in range(LOCAL):
        asked = jnp.where(at == one, owner_ref[one], asked)
    asked = asked.astype(jnp.float32).astype(jnp.bfloat16)
    for prompt in range(PROMPTS):
        which, head = column_of(prompt // 2 % 4)
        source = value_ref if which else key_ref
        for lane in range(LANES):
            first = (lane * KV_LANE + head) * HD
            out_ref[prompt * LANES + lane] = jnp.concatenate(
                [source[:, first : first + HD], asked], 0
            )


def pick_kernel(pieces_ref, out_ref, owner_ref, owners, sem):
    resp = lax.axis_index("resp")
    prompt = resp // 4
    turn = (resp % 4 + LANES - lax.axis_index("tp")) % 4
    for x in range(4):
        for block in range(4):
            source = (prompt // 8 * 8 + x * 2 + prompt % 2) * LANES + (block + 4 - turn) % 4
            tile = pieces_ref[source].astype(jnp.float32)
            owner_ref[x * 4 + block : x * 4 + block + 1] = tile[TILE : TILE + 1].astype(jnp.int32)
    copy = pltpu.make_async_copy(owner_ref, owners, sem)
    copy.start()
    copy.wait()
    for member in range(MEMBERS):
        for one in range(LOCAL):
            owner = owners[member, one]
            for lane in range(LANES):
                out_ref[member, one, lane * TILE : (lane + 1) * TILE] = pieces_ref[
                    owner * LANES + lane, :TILE
                ]


def fold_kernel(owner_ref, terms_ref, token_ref, out_ref, total):
    total[...] = jnp.zeros_like(total)
    for one in range(LOCAL):
        for member in range(MEMBERS):
            owner = owner_ref[member, one]
            total[owner] += terms_ref[member, one].astype(jnp.float32)
    for prompt in range(PROMPTS):
        for lane in range(LANES):
            out_ref[prompt * LANES + lane] = total[
                prompt, lane * TILE : (lane + 1) * TILE
            ].astype(out_ref.dtype)


def summed_kernel(sums_ref, token_ref, key_ref, value_ref):
    for x in range(4):
        which, head = column_of(x)
        target = value_ref if which else key_ref
        for lane in range(LANES):
            tile = jnp.zeros((TILE, HD), jnp.float32)
            for z in range(2):
                for high in range(2):
                    source = (z * 8 + x * 2 + high) * LANES + lane
                    tile = tile + sums_ref[source].astype(jnp.float32)
            first = (lane * KV_LANE + head) * HD
            target[:, first : first + HD] = tile.astype(target.dtype)


def stacked(ref, head, first):
    parts = [ref[first : first + ROWS, column] for _, column in heads(head)]
    return jnp.concatenate(parts, 0)


def heads(head):
    for at in range(PER_GROUP):
        column = (head * PER_GROUP + at) * HD
        yield slice(at * ROWS, (at + 1) * ROWS), slice(column, column + HD)


def by_length(length, span, work, blank):
    for first in range(0, span, 2 * ROWS):
        second = first + ROWS
        last = min(second + ROWS, span)
        if second < span:

            @pl.when(length > second)
            def _():
                work((first, second))

        @pl.when((length > first) & ((length <= second) | (second >= span)))
        def _():
            work((first,))
            if second < span:
                blank(second, last)

        @pl.when(length <= first)
        def _():
            blank(first, last)


def kept_copies(kept, held, sems, response, slot, head, first, out):
    chunk = first // ROWS
    rows = pl.ds(0, LP + first + ROWS)
    for at in range(2):
        far = kept.at[response, at, head, chunk, rows]
        near = held[at].at[slot, head, chunk, rows]
        source, target = (near, far) if out else (far, near)
        yield pltpu.make_async_copy(source, target, sems.at[slot, head, chunk, at])


def each_live(length_ref, start, count, span, act):
    for slot in range(count):
        for first in range(0, span, ROWS):

            @pl.when(length_ref[start + slot] > first)
            def _():
                for head in range(KV_LANE):
                    act(start + slot, slot, head, first)


def attend_kernel(
    length_ref,
    query_ref,
    grad_ref,
    key_ref,
    value_ref,
    prompt_ref,
    prompt_grad_ref,
    kept,
    keys,
    values,
    scores,
    prob_grads,
    probability_ref,
    score_grad_ref,
    key_total,
    value_total,
    sems,
):
    held = (probability_ref, score_grad_ref)
    response = pl.program_id(0)
    length = length_ref[response]
    span = key_ref.shape[0]
    scale = HD**-0.5
    wide = PER_GROUP * ROWS
    for head in range(KV_LANE):
        for whole, own_ref, which in ((keys, key_ref, 0), (values, value_ref, 1)):
            whole[head, :LP] = prompt_ref[which, head, :, 0].reshape(LP, HD)
            whole[head, LP:] = own_ref[:, head * HD : (head + 1) * HD]

    def score(slot, head, first):
        count = LP + first + ROWS
        lane = lax.broadcasted_iota(jnp.int32, (1, wide), 1) % ROWS
        causal = lax.broadcasted_iota(jnp.int32, (ROWS, 1), 0) <= lane
        raw = lax.dot_general(
            keys[head, :count],
            stacked(query_ref, head, first),
            (((1,), (1,)), ((), ())),
            preferred_element_type=jnp.float32,
        )
        tail = jnp.where(causal, raw[count - ROWS :], -1e30)
        scores[slot, : count - ROWS] = raw[: count - ROWS]
        scores[slot, count - ROWS : count] = tail
        top = jnp.max(raw[: count - ROWS].reshape(-1, 8, wide), axis=0)
        top = jnp.maximum(top, jnp.max(tail.reshape(-1, 8, wide), axis=0))
        prob_grads[slot, :count] = lax.dot_general(
            values[head, :count],
            stacked(grad_ref, head, first),
            (((1,), (1,)), ((), ())),
            preferred_element_type=jnp.float32,
        )
        return jnp.max(top, axis=0, keepdims=True) * (scale * LOG2E)

    def soften(slot, head, first, largest):
        count = LP + first + ROWS
        chunk = first // ROWS
        lane = lax.broadcasted_iota(jnp.int32, (1, wide), 1) % ROWS
        live = first + lane < length
        blocks = [slice(at, at + ROWS) for at in range(0, count, ROWS)]
        total = jnp.zeros((8, wide), jnp.float32)
        moved = jnp.zeros((8, wide), jnp.float32)
        for block in blocks:
            weights = jnp.exp2(scores[slot, block] * (scale * LOG2E) - largest)
            scores[slot, block] = weights
            total = total + jnp.sum(weights.reshape(-1, 8, wide), axis=0)
            terms = weights * prob_grads[slot, block]
            moved = moved + jnp.sum(terms.reshape(-1, 8, wide), axis=0)
        inverse = jnp.where(live, 1.0 / jnp.sum(total, axis=0, keepdims=True), 0.0)
        delta = jnp.sum(moved, axis=0, keepdims=True) * inverse
        for block in blocks:
            probability = scores[slot, block] * inverse
            probability_ref[response, head, chunk, block] = probability.astype(jnp.bfloat16)
            score_grad_ref[response, head, chunk, block] = (
                probability * (prob_grads[slot, block] - delta)
            ).astype(jnp.bfloat16)

    def gather(head, first):
        for total, left_ref, right_ref in (
            (value_total, probability_ref, grad_ref),
            (key_total, score_grad_ref, query_ref),
        ):
            terms = jnp.dot(
                left_ref[response, head, first // ROWS, :LP],
                stacked(right_ref, head, first),
                preferred_element_type=jnp.float32,
            )
            if first == 0:
                total[head] = terms
            else:
                total[head] += terms

    def work(firsts):
        streams = [(head, first) for first in firsts for head in range(KV_LANE)]
        largest = {0: score(0, *streams[0])}
        for slot, stream in enumerate(streams):
            if slot + 1 < len(streams):
                largest[slot + 1] = score(slot + 1, *streams[slot + 1])
            soften(slot, *stream, largest[slot])
            for copy in kept_copies(kept, held, sems, response, response, *stream, True):
                copy.start()
            gather(*stream)

    by_length(length, span, work, lambda first, last: None)

    for head in range(KV_LANE):
        key_terms = (key_total[head] * scale).astype(jnp.bfloat16)
        value_terms = value_total[head].astype(jnp.bfloat16)
        prompt_grad_ref[0, head, :, 0] = key_terms.reshape(GROUPS, SLICE, HD)
        prompt_grad_ref[1, head, :, 0] = value_terms.reshape(GROUPS, SLICE, HD)

    def finish(*chunk):
        for copy in kept_copies(kept, held, sems, *chunk, True):
            copy.wait()

    @pl.when(response == LOCAL - 1)
    def _():
        each_live(length_ref, 0, LOCAL, span, finish)


def outputs_kernel(
    start, length_ref, query_ref, grad_ref, key_ref, value_ref, prompt_ref, kept, *rest
):
    out_ref, query_grad_ref, key_grad_ref, value_grad_ref, token_ref, *rest = rest[-12:]
    keys_t, values_t, probability_ref, score_grad_ref, key_total, value_total, sems = rest
    held = (probability_ref, score_grad_ref)
    slot = pl.program_id(0)
    response = start + slot
    length = length_ref[response]
    span = out_ref.shape[0]
    scale = HD**-0.5

    def fetch(*chunk):
        for copy in kept_copies(kept, held, sems, *chunk, False):
            copy.start()

    @pl.when(slot == 0)
    def _():
        each_live(length_ref, start, HALF, span, fetch)

    for head in range(KV_LANE):
        lanes = slice(head * HD, (head + 1) * HD)
        for whole_t, own_ref, which in ((keys_t, key_ref, 0), (values_t, value_ref, 1)):
            whole_t[head] = jnp.concatenate(
                [prompt_ref[which, head, :, 0].reshape(LP, HD), own_ref[:, lanes]], 0
            ).T

    def work(firsts):
        for first in firsts:
            count = LP + first + ROWS
            chunk = first // ROWS
            rows = slice(first, first + ROWS)
            for head in range(KV_LANE):
                for copy in kept_copies(kept, held, sems, response, slot, head, first, False):
                    copy.wait()
            for head in range(KV_LANE):
                output = jnp.dot(
                    values_t[head, :, :count],
                    probability_ref[slot, head, chunk, :count],
                    preferred_element_type=jnp.float32,
                )
                query_grad = jnp.dot(
                    keys_t[head, :, :count],
                    score_grad_ref[slot, head, chunk, :count],
                    preferred_element_type=jnp.float32,
                )
                output = output.astype(jnp.bfloat16).T
                query_grad = (query_grad * scale).astype(jnp.bfloat16).T
                for part, column in heads(head):
                    out_ref[rows, column] = output[part]
                    query_grad_ref[rows, column] = query_grad[part]
                for total, left_ref, right_ref in (
                    (value_total, probability_ref, grad_ref),
                    (key_total, score_grad_ref, query_ref),
                ):
                    terms = jnp.dot(
                        left_ref[slot, head, chunk, LP:count],
                        stacked(right_ref, head, first),
                        preferred_element_type=jnp.float32,
                    )
                    if first > 0:
                        total[head, :first] += terms[:first]
                    total[head, rows] = terms[first:]

    def blank(first, last):
        zeros = jnp.zeros((last - first, out_ref.shape[1]), jnp.bfloat16)
        out_ref[first:last, :] = zeros
        query_grad_ref[first:last, :] = zeros
        zeros = jnp.zeros((KV_LANE, last - first, HD), jnp.float32)
        key_total[:, first:last] = zeros
        value_total[:, first:last] = zeros

    by_length(length, span, work, blank)
    for head in range(KV_LANE):
        lanes = slice(head * HD, (head + 1) * HD)
        key_grad_ref[:, lanes] = (key_total[head] * scale).astype(jnp.bfloat16)
        value_grad_ref[:, lanes] = value_total[head].astype(jnp.bfloat16)
    token_ref[...] = jnp.zeros_like(token_ref)


def specs(span, wide, narrow, start=0):
    return dict(
        wide=pl.BlockSpec((span, wide), lambda i, length: (start + i, 0)),
        narrow=pl.BlockSpec((span, narrow), lambda i, length: (start + i, 0)),
        prompt=pl.BlockSpec(
            (2, KV_LANE, GROUPS, 1, SLICE, HD), lambda i, length: (0, 0, 0, start + i, 0, 0)
        ),
        kept=pl.BlockSpec(memory_space=pl.ANY),
    )


def attend(lengths, queries, out_grad, resp_keys, resp_values, prompt_rows):
    count = lengths.shape[0]
    span = queries.shape[0] // count
    both = LP + span
    streams = 2 * KV_LANE
    wide = PER_GROUP * ROWS
    spec = specs(span, queries.shape[1], resp_keys.shape[1])
    held = (count, KV_LANE, CHUNKS, both, wide)
    return pl.pallas_call(
        attend_kernel,
        out_shape=(
            jax.ShapeDtypeStruct(prompt_rows.shape, jnp.bfloat16),
            jax.ShapeDtypeStruct((count, 2, KV_LANE, CHUNKS, both, wide), jnp.bfloat16),
        ),
        grid_spec=pltpu.PrefetchScalarGridSpec(
            num_scalar_prefetch=1,
            grid=(count,),
            in_specs=[spec[name] for name in ("wide", "wide", "narrow", "narrow", "prompt")],
            out_specs=[spec[name] for name in ("prompt", "kept")],
            scratch_shapes=[
                pltpu.VMEM((KV_LANE, both, HD), jnp.bfloat16),
                pltpu.VMEM((KV_LANE, both, HD), jnp.bfloat16),
                pltpu.VMEM((streams, both, wide), jnp.float32),
                pltpu.VMEM((streams, both, wide), jnp.float32),
                pltpu.VMEM(held, jnp.bfloat16),
                pltpu.VMEM(held, jnp.bfloat16),
                pltpu.VMEM((KV_LANE, LP, HD), jnp.float32),
                pltpu.VMEM((KV_LANE, LP, HD), jnp.float32),
                pltpu.SemaphoreType.DMA((count, KV_LANE, CHUNKS, 2)),
            ],
        ),
        compiler_params=LARGE,
        cost_estimate=pl.CostEstimate(
            flops=16 * queries.size * both,
            bytes_accessed=4 * queries.size,
            transcendentals=queries.size * both // HD,
        ),
    )(lengths, queries, out_grad, resp_keys, resp_values, prompt_rows)


def outputs(
    lengths, queries, out_grad, resp_keys, resp_values, prompt_rows, kept, start=0, earlier=()
):
    rows, wide = queries.shape
    span = rows // lengths.shape[0]
    both = LP + span
    spec = specs(span, wide, resp_keys.shape[1], start)
    held = (HALF, KV_LANE, CHUNKS, both, PER_GROUP * ROWS)
    shape = jax.ShapeDtypeStruct(queries.shape, jnp.bfloat16)
    own = jax.ShapeDtypeStruct(resp_keys.shape, jnp.bfloat16)
    return pl.pallas_call(
        functools.partial(outputs_kernel, start),
        out_shape=(shape, shape, own, own, jax.ShapeDtypeStruct((8, HD), jnp.int32)),
        grid_spec=pltpu.PrefetchScalarGridSpec(
            num_scalar_prefetch=1,
            grid=(HALF,),
            in_specs=[spec[name] for name in ("wide", "wide", "narrow", "narrow", "prompt", "kept")]
            + [spec["kept"]] * len(earlier),
            out_specs=[
                spec["wide"],
                spec["wide"],
                spec["narrow"],
                spec["narrow"],
                pl.BlockSpec((8, HD), lambda i, length: (0, 0)),
            ],
            scratch_shapes=[
                pltpu.VMEM((KV_LANE, HD, both), jnp.bfloat16),
                pltpu.VMEM((KV_LANE, HD, both), jnp.bfloat16),
                pltpu.VMEM(held, jnp.bfloat16),
                pltpu.VMEM(held, jnp.bfloat16),
                pltpu.VMEM((KV_LANE, span, HD), jnp.float32),
                pltpu.VMEM((KV_LANE, span, HD), jnp.float32),
                pltpu.SemaphoreType.DMA((HALF, KV_LANE, CHUNKS, 2)),
            ],
        ),
        input_output_aliases={7 + at: at for at in range(len(earlier[:4]))},
        compiler_params=LARGE,
        cost_estimate=pl.CostEstimate(
            flops=4 * rows * wide * both,
            bytes_accessed=2 * rows * wide + kept.size,
            transcendentals=0,
        ),
    )(lengths, queries, out_grad, resp_keys, resp_values, prompt_rows, kept, *earlier)


def whole(kernel, out_shape, spaces, *operands, params=SMALL, **more):
    return pl.pallas_call(
        kernel,
        out_shape=out_shape,
        in_specs=[pl.BlockSpec(memory_space=space) for space in spaces],
        compiler_params=params,
        **more,
    )(*operands)


def low(*shape):
    return jax.ShapeDtypeStruct(shape, jnp.bfloat16)


def shards(
    queries, resp_keys, resp_values, out_grad, prompt_keys, prompt_values, lengths, prompt_of
):
    pieces = over_store(
        whole(
            stored_kernel,
            low(PROMPTS * LANES, SENT, HD),
            [pltpu.HBM] * 3,
            prompt_of,
            prompt_keys,
            prompt_values,
            params=FIRST,
            scratch_shapes=[
                pltpu.SMEM(prompt_of.shape, jnp.int32),
                pltpu.VMEM(prompt_keys.shape, jnp.bfloat16),
                pltpu.VMEM(prompt_values.shape, jnp.bfloat16),
                pltpu.SemaphoreType.DMA((3,)),
            ],
        )
    )
    picked, owners = whole(
        pick_kernel,
        (low(MEMBERS, LOCAL, SLICE, HD), jax.ShapeDtypeStruct((MEMBERS, HD), jnp.int32)),
        [pltpu.VMEM],
        pieces,
        scratch_shapes=[pltpu.SMEM((MEMBERS, HD), jnp.int32), pltpu.SemaphoreType.DMA],
    )
    prompt_rows = over_pick(picked).reshape(2, KV_LANE, GROUPS, LOCAL, SLICE, HD)
    shared = (lengths, queries, out_grad, resp_keys, resp_values, prompt_rows)
    terms, kept = attend(*shared)
    terms = over_pick(terms.reshape(MEMBERS, LOCAL, SLICE, HD))
    *results, token = outputs(*shared, kept)
    sums = whole(
        fold_kernel,
        low(PROMPTS * LANES, TILE, HD),
        [pltpu.SMEM, pltpu.VMEM, pl.ANY],
        owners,
        terms,
        token,
        scratch_shapes=[pltpu.VMEM((PROMPTS, SLICE, HD), jnp.float32)],
    )
    *results, token = outputs(*shared, kept, HALF, (*results, sums))
    prompt_key_grad, prompt_value_grad = whole(
        summed_kernel,
        (low(*prompt_keys.shape), low(*prompt_values.shape)),
        [pltpu.VMEM, pl.ANY],
        over_store(sums),
        token,
    )
    return (*results, prompt_key_grad, prompt_value_grad)


def solution(mesh):
    wide = P("resp", "tp")
    stored = P(("resp", "tp"), None)
    return jax.shard_map(
        shards,
        mesh=mesh,
        in_specs=(wide, wide, wide, wide, stored, stored, P("resp"), P("resp")),
        out_specs=(wide, wide, wide, wide, stored, stored),
        check_vma=False,
    )
```

```python
import functools

import jax
import jax.numpy as jnp
from jax import lax
from jax.experimental import pallas as pl
from jax.experimental.pallas import tpu as pltpu
from jax.sharding import PartitionSpec as P

HD = 128
LP = 256
ROWS = 32
PER_GROUP = 8
KV_LANE = 2
LANES = 4
GROUPS = 4
TILE = 16
MEMBERS = 16
PROMPTS = 16
LOCAL = 4
SLICE = LP // GROUPS
CHUNKS = 5
HALF = LOCAL // 2
SENT = TILE + 8
LOG2E = 1.4426950408889634
LARGE = pltpu.CompilerParams(vmem_limit_bytes=48 * 1024 * 1024)
FIRST = pltpu.CompilerParams(vmem_limit_bytes=(64 * 1024 - 64) * 1024)
STACK = pltpu.CompilerParams(vmem_limit_bytes=55 * 1024 * 1024)
ATTEND = pltpu.CompilerParams(vmem_limit_bytes=62 * 1024 * 1024)
SMALL = pltpu.CompilerParams(vmem_limit_bytes=16 * 1024 * 1024)

STORE_GROUPS = [
    [(p * 4 + (turn + t) % 4) * 4 + t for p in range(PROMPTS) for t in range(LANES)]
    for turn in range(4)
]
PICK_GROUPS = [
    [z * 32 + x * 8 + high * 4 + block for x in range(4) for block in range(4)]
    for z in range(2)
    for high in range(2)
]


def over_store(array):
    return lax.all_to_all(
        array,
        ("resp", "tp"),
        split_axis=0,
        concat_axis=0,
        tiled=True,
        axis_index_groups=STORE_GROUPS,
    )


def over_pick(array):
    return lax.all_to_all(
        array, "resp", split_axis=0, concat_axis=0, tiled=True, axis_index_groups=PICK_GROUPS
    )


def column_of(x):
    return (x // KV_LANE, x % KV_LANE)


def stored_kernel(
    owner_hbm, key_hbm, value_hbm, out_ref, owner_ref, key_ref, value_ref, sems
):
    copies = [
        pltpu.make_async_copy(source, target, sems.at[at])
        for at, (source, target) in enumerate(
            ((owner_hbm, owner_ref), (key_hbm, key_ref), (value_hbm, value_ref))
        )
    ]
    for copy in copies:
        copy.start()
    for copy in copies:
        copy.wait()
    at = lax.broadcasted_iota(jnp.int32, (SENT - TILE, HD), 1)
    asked = jnp.zeros((SENT - TILE, HD), jnp.int32)
    for one in range(LOCAL):
        asked = jnp.where(at == one, owner_ref[one], asked)
    asked = asked.astype(jnp.float32).astype(jnp.bfloat16)
    for prompt in range(PROMPTS):
        which, head = column_of(prompt // 2 % 4)
        source = value_ref if which else key_ref
        for lane in range(LANES):
            first = (lane * KV_LANE + head) * HD
            out_ref[prompt * LANES + lane] = jnp.concatenate(
                [source[:, first : first + HD], asked], 0
            )


def pick_kernel(pieces_ref, token_ref, out_ref, owner_ref, owners, sem):
    resp = lax.axis_index("resp")
    prompt = resp // 4
    turn = (resp % 4 + LANES - lax.axis_index("tp")) % 4
    for x in range(4):
        for block in range(4):
            source = (prompt // 8 * 8 + x * 2 + prompt % 2) * LANES + (block + 4 - turn) % 4
            tile = pieces_ref[source].astype(jnp.float32)
            owner_ref[x * 4 + block : x * 4 + block + 1] = tile[TILE : TILE + 1].astype(jnp.int32)
    copy = pltpu.make_async_copy(owner_ref, owners, sem)
    copy.start()
    copy.wait()
    for member in range(MEMBERS):
        for one in range(LOCAL):
            owner = owners[member, one]
            for lane in range(LANES):
                out_ref[member, one, lane * TILE : (lane + 1) * TILE] = pieces_ref[
                    owner * LANES + lane, :TILE
                ]


def fold_kernel(owner_ref, terms_ref, token_ref, out_ref, total):
    total[...] = jnp.zeros_like(total)
    for one in range(LOCAL):
        for member in range(MEMBERS):
            owner = owner_ref[member, one]
            total[owner] += terms_ref[member, one].astype(jnp.float32)
    for prompt in range(PROMPTS):
        for lane in range(LANES):
            out_ref[prompt * LANES + lane] = total[
                prompt, lane * TILE : (lane + 1) * TILE
            ].astype(out_ref.dtype)


def summed_kernel(sums_ref, token_ref, key_ref, value_ref):
    for x in range(4):
        which, head = column_of(x)
        target = value_ref if which else key_ref
        for lane in range(LANES):
            tile = jnp.zeros((TILE, HD), jnp.float32)
            for z in range(2):
                for high in range(2):
                    source = (z * 8 + x * 2 + high) * LANES + lane
                    tile = tile + sums_ref[source].astype(jnp.float32)
            first = (lane * KV_LANE + head) * HD
            target[:, first : first + HD] = tile.astype(target.dtype)


def stacked(ref, head, first):
    return ref[0, head, first // ROWS]


def heads(head):
    for at in range(PER_GROUP):
        column = (head * PER_GROUP + at) * HD
        yield slice(at * ROWS, (at + 1) * ROWS), slice(column, column + HD)


def stack_kernel(query_ref, grad_ref, stacked_query, stacked_grad, token_ref):
    for chunk in range(CHUNKS):
        rows = slice(chunk * ROWS, (chunk + 1) * ROWS)
        for head in range(KV_LANE):
            for part, column in heads(head):
                stacked_query[0, head, chunk, part] = query_ref[rows, column]
                stacked_grad[0, head, chunk, part] = grad_ref[rows, column]
    token_ref[...] = jnp.zeros_like(token_ref)


def by_length(length, span, work, blank):
    for first in range(0, span, 2 * ROWS):
        second = first + ROWS
        last = min(second + ROWS, span)
        if second < span:

            @pl.when(length > second)
            def _():
                work((first, second))

        @pl.when((length > first) & ((length <= second) | (second >= span)))
        def _():
            work((first,))
            if second < span:
                blank(second, last)

        @pl.when(length <= first)
        def _():
            blank(first, last)


def kept_copies(kept, held, sems, response, slot, head, first, out):
    chunk = first // ROWS
    rows = pl.ds(0, LP + first + ROWS)
    for at in range(2):
        far = kept.at[response, at, head, chunk, rows]
        near = held[at].at[slot, head, chunk, rows]
        source, target = (near, far) if out else (far, near)
        yield pltpu.make_async_copy(source, target, sems.at[slot, head, chunk, at])


def each_live(length_ref, start, count, span, act):
    for slot in range(count):
        for first in range(0, span, ROWS):

            @pl.when(length_ref[start + slot] > first)
            def _():
                for head in range(KV_LANE):
                    act(start + slot, slot, head, first)


def attend_kernel(
    length_ref,
    query_ref,
    grad_ref,
    key_ref,
    value_ref,
    prompt_ref,
    prompt_grad_ref,
    kept,
    keys,
    values,
    scores,
    prob_grads,
    probability_ref,
    score_grad_ref,
    key_total,
    value_total,
    sems,
):
    held = (probability_ref, score_grad_ref)
    response = pl.program_id(0)
    length = length_ref[response]
    span = key_ref.shape[0]
    scale = HD**-0.5
    wide = PER_GROUP * ROWS
    for head in range(KV_LANE):
        for whole, own_ref, which in ((keys, key_ref, 0), (values, value_ref, 1)):
            whole[head, :LP] = prompt_ref[which, head, :, 0].reshape(LP, HD)
            whole[head, LP:] = own_ref[:, head * HD : (head + 1) * HD]

    def score(slot, head, first):
        count = LP + first + ROWS
        lane = lax.broadcasted_iota(jnp.int32, (1, wide), 1) % ROWS
        causal = lax.broadcasted_iota(jnp.int32, (ROWS, 1), 0) <= lane
        raw = lax.dot_general(
            keys[head, :count],
            stacked(query_ref, head, first),
            (((1,), (1,)), ((), ())),
            preferred_element_type=jnp.float32,
        )
        tail = jnp.where(causal, raw[count - ROWS :], -1e30)
        scores[slot, : count - ROWS] = raw[: count - ROWS]
        scores[slot, count - ROWS : count] = tail
        top = jnp.max(raw[: count - ROWS].reshape(-1, 8, wide), axis=0)
        top = jnp.maximum(top, jnp.max(tail.reshape(-1, 8, wide), axis=0))
        prob_grads[slot, :count] = lax.dot_general(
            values[head, :count],
            stacked(grad_ref, head, first),
            (((1,), (1,)), ((), ())),
            preferred_element_type=jnp.float32,
        )
        return jnp.max(top, axis=0, keepdims=True) * (scale * LOG2E)

    def soften(slot, head, first, largest):
        count = LP + first + ROWS
        chunk = first // ROWS
        lane = lax.broadcasted_iota(jnp.int32, (1, wide), 1) % ROWS
        live = first + lane < length
        blocks = [slice(at, at + ROWS) for at in range(0, count, ROWS)]
        total = jnp.zeros((8, wide), jnp.float32)
        moved = jnp.zeros((8, wide), jnp.float32)
        for block in blocks:
            weights = jnp.exp2(scores[slot, block] * (scale * LOG2E) - largest)
            scores[slot, block] = weights
            total = total + jnp.sum(weights.reshape(-1, 8, wide), axis=0)
            terms = weights * prob_grads[slot, block]
            moved = moved + jnp.sum(terms.reshape(-1, 8, wide), axis=0)
        inverse = jnp.where(live, 1.0 / jnp.sum(total, axis=0, keepdims=True), 0.0)
        delta = jnp.sum(moved, axis=0, keepdims=True) * inverse
        for block in blocks:
            probability = scores[slot, block] * inverse
            probability_ref[response, head, chunk, block] = probability.astype(jnp.bfloat16)
            score_grad_ref[response, head, chunk, block] = (
                probability * (prob_grads[slot, block] - delta)
            ).astype(jnp.bfloat16)

    def gather(head, first):
        for total, left_ref, right_ref in (
            (value_total, probability_ref, grad_ref),
            (key_total, score_grad_ref, query_ref),
        ):
            terms = jnp.dot(
                left_ref[response, head, first // ROWS, :LP],
                stacked(right_ref, head, first),
                preferred_element_type=jnp.float32,
            )
            if first == 0:
                total[head] = terms
            else:
                total[head] += terms

    def work(firsts):
        streams = [(head, first) for first in firsts for head in range(KV_LANE)]
        largest = {0: score(0, *streams[0])}
        for slot, stream in enumerate(streams):
            if slot + 1 < len(streams):
                largest[slot + 1] = score(slot + 1, *streams[slot + 1])
            soften(slot, *stream, largest[slot])
            for copy in kept_copies(kept, held, sems, response, response, *stream, True):
                copy.start()
            gather(*stream)

    by_length(length, span, work, lambda first, last: None)

    for head in range(KV_LANE):
        key_terms = (key_total[head] * scale).astype(jnp.bfloat16)
        value_terms = value_total[head].astype(jnp.bfloat16)
        prompt_grad_ref[0, head, :, 0] = key_terms.reshape(GROUPS, SLICE, HD)
        prompt_grad_ref[1, head, :, 0] = value_terms.reshape(GROUPS, SLICE, HD)

    def finish(*chunk):
        for copy in kept_copies(kept, held, sems, *chunk, True):
            copy.wait()

    @pl.when(response == LOCAL - 1)
    def _():
        each_live(length_ref, 0, LOCAL, span, finish)


def outputs_kernel(
    start, length_ref, query_ref, grad_ref, key_ref, value_ref, prompt_ref, kept, *rest
):
    out_ref, query_grad_ref, key_grad_ref, value_grad_ref, token_ref, *rest = rest[-12:]
    keys_t, values_t, probability_ref, score_grad_ref, key_total, value_total, sems = rest
    held = (probability_ref, score_grad_ref)
    slot = pl.program_id(0)
    response = start + slot
    length = length_ref[response]
    span = out_ref.shape[0]
    scale = HD**-0.5

    def fetch(*chunk):
        for copy in kept_copies(kept, held, sems, *chunk, False):
            copy.start()

    @pl.when(slot == 0)
    def _():
        each_live(length_ref, start, HALF, span, fetch)

    for head in range(KV_LANE):
        lanes = slice(head * HD, (head + 1) * HD)
        for whole_t, own_ref, which in ((keys_t, key_ref, 0), (values_t, value_ref, 1)):
            whole_t[head] = jnp.concatenate(
                [prompt_ref[which, head, :, 0].reshape(LP, HD), own_ref[:, lanes]], 0
            ).T

    def work(firsts):
        for first in firsts:
            count = LP + first + ROWS
            chunk = first // ROWS
            rows = slice(first, first + ROWS)
            for head in range(KV_LANE):
                for copy in kept_copies(kept, held, sems, response, slot, head, first, False):
                    copy.wait()
            for head in range(KV_LANE):
                output = jnp.dot(
                    values_t[head, :, :count],
                    probability_ref[slot, head, chunk, :count],
                    preferred_element_type=jnp.float32,
                )
                query_grad = jnp.dot(
                    keys_t[head, :, :count],
                    score_grad_ref[slot, head, chunk, :count],
                    preferred_element_type=jnp.float32,
                )
                output = output.astype(jnp.bfloat16).T
                query_grad = (query_grad * scale).astype(jnp.bfloat16).T
                for part, column in heads(head):
                    out_ref[rows, column] = output[part]
                    query_grad_ref[rows, column] = query_grad[part]
                for total, left_ref, right_ref in (
                    (value_total, probability_ref, grad_ref),
                    (key_total, score_grad_ref, query_ref),
                ):
                    terms = jnp.dot(
                        left_ref[slot, head, chunk, LP:count],
                        stacked(right_ref, head, first),
                        preferred_element_type=jnp.float32,
                    )
                    if first > 0:
                        total[head, :first] += terms[:first]
                    total[head, rows] = terms[first:]

    def blank(first, last):
        zeros = jnp.zeros((last - first, out_ref.shape[1]), jnp.bfloat16)
        out_ref[first:last, :] = zeros
        query_grad_ref[first:last, :] = zeros
        zeros = jnp.zeros((KV_LANE, last - first, HD), jnp.float32)
        key_total[:, first:last] = zeros
        value_total[:, first:last] = zeros

    by_length(length, span, work, blank)
    for head in range(KV_LANE):
        lanes = slice(head * HD, (head + 1) * HD)
        key_grad_ref[:, lanes] = (key_total[head] * scale).astype(jnp.bfloat16)
        value_grad_ref[:, lanes] = value_total[head].astype(jnp.bfloat16)
    token_ref[...] = jnp.zeros_like(token_ref)


def specs(span, wide, narrow, start=0):
    return dict(
        wide=pl.BlockSpec((span, wide), lambda i, length: (start + i, 0)),
        rows=pl.BlockSpec(
            (1, KV_LANE, CHUNKS, PER_GROUP * ROWS, HD), lambda i, length: (start + i, 0, 0, 0, 0)
        ),
        narrow=pl.BlockSpec((span, narrow), lambda i, length: (start + i, 0)),
        prompt=pl.BlockSpec(
            (2, KV_LANE, GROUPS, 1, SLICE, HD), lambda i, length: (0, 0, 0, start + i, 0, 0)
        ),
        kept=pl.BlockSpec(memory_space=pl.ANY),
    )


def stack(queries, out_grad, count):
    span = queries.shape[0] // count
    block = (1, KV_LANE, CHUNKS, PER_GROUP * ROWS, HD)
    shape = jax.ShapeDtypeStruct((count,) + block[1:], jnp.bfloat16)
    wide = pl.BlockSpec((span, queries.shape[1]), lambda i: (i, 0))
    rows = pl.BlockSpec(block, lambda i: (i, 0, 0, 0, 0))
    return pl.pallas_call(
        stack_kernel,
        out_shape=(shape, shape, jax.ShapeDtypeStruct((8, HD), jnp.int32)),
        grid=(count,),
        in_specs=[wide, wide],
        out_specs=[rows, rows, pl.BlockSpec((8, HD), lambda i: (0, 0))],
        compiler_params=STACK,
        cost_estimate=pl.CostEstimate(
            flops=0, bytes_accessed=8 * queries.size, transcendentals=0
        ),
    )(queries, out_grad)


def attend(lengths, queries, out_grad, resp_keys, resp_values, prompt_rows):
    count = lengths.shape[0]
    span = resp_keys.shape[0] // count
    both = LP + span
    streams = 2 * KV_LANE
    wide = PER_GROUP * ROWS
    spec = specs(span, queries.size // resp_keys.shape[0], resp_keys.shape[1])
    held = (count, KV_LANE, CHUNKS, both, wide)
    return pl.pallas_call(
        attend_kernel,
        out_shape=(
            jax.ShapeDtypeStruct(prompt_rows.shape, jnp.bfloat16),
            jax.ShapeDtypeStruct((count, 2, KV_LANE, CHUNKS, both, wide), jnp.bfloat16),
        ),
        grid_spec=pltpu.PrefetchScalarGridSpec(
            num_scalar_prefetch=1,
            grid=(count,),
            in_specs=[spec[name] for name in ("rows", "rows", "narrow", "narrow", "prompt")],
            out_specs=[spec[name] for name in ("prompt", "kept")],
            scratch_shapes=[
                pltpu.VMEM((KV_LANE, both, HD), jnp.bfloat16),
                pltpu.VMEM((KV_LANE, both, HD), jnp.bfloat16),
                pltpu.VMEM((streams, both, wide), jnp.float32),
                pltpu.VMEM((streams, both, wide), jnp.float32),
                pltpu.VMEM(held, jnp.bfloat16),
                pltpu.VMEM(held, jnp.bfloat16),
                pltpu.VMEM((KV_LANE, LP, HD), jnp.float32),
                pltpu.VMEM((KV_LANE, LP, HD), jnp.float32),
                pltpu.SemaphoreType.DMA((count, KV_LANE, CHUNKS, 2)),
            ],
        ),
        compiler_params=ATTEND,
        cost_estimate=pl.CostEstimate(
            flops=16 * queries.size * both,
            bytes_accessed=4 * queries.size,
            transcendentals=queries.size * both // HD,
        ),
    )(lengths, queries, out_grad, resp_keys, resp_values, prompt_rows)


def outputs(
    lengths, queries, out_grad, resp_keys, resp_values, prompt_rows, kept, start=0, earlier=()
):
    rows = resp_keys.shape[0]
    wide = queries.size // rows
    span = rows // lengths.shape[0]
    both = LP + span
    spec = specs(span, wide, resp_keys.shape[1], start)
    held = (HALF, KV_LANE, CHUNKS, both, PER_GROUP * ROWS)
    shape = jax.ShapeDtypeStruct((rows, wide), jnp.bfloat16)
    own = jax.ShapeDtypeStruct(resp_keys.shape, jnp.bfloat16)
    return pl.pallas_call(
        functools.partial(outputs_kernel, start),
        out_shape=(shape, shape, own, own, jax.ShapeDtypeStruct((8, HD), jnp.int32)),
        grid_spec=pltpu.PrefetchScalarGridSpec(
            num_scalar_prefetch=1,
            grid=(HALF,),
            in_specs=[spec[name] for name in ("rows", "rows", "narrow", "narrow", "prompt", "kept")]
            + [spec["kept"]] * len(earlier),
            out_specs=[
                spec["wide"],
                spec["wide"],
                spec["narrow"],
                spec["narrow"],
                pl.BlockSpec((8, HD), lambda i, length: (0, 0)),
            ],
            scratch_shapes=[
                pltpu.VMEM((KV_LANE, HD, both), jnp.bfloat16),
                pltpu.VMEM((KV_LANE, HD, both), jnp.bfloat16),
                pltpu.VMEM(held, jnp.bfloat16),
                pltpu.VMEM(held, jnp.bfloat16),
                pltpu.VMEM((KV_LANE, span, HD), jnp.float32),
                pltpu.VMEM((KV_LANE, span, HD), jnp.float32),
                pltpu.SemaphoreType.DMA((HALF, KV_LANE, CHUNKS, 2)),
            ],
        ),
        input_output_aliases={7 + at: at for at in range(len(earlier[:4]))},
        compiler_params=LARGE,
        cost_estimate=pl.CostEstimate(
            flops=4 * rows * wide * both,
            bytes_accessed=2 * rows * wide + kept.size,
            transcendentals=0,
        ),
    )(lengths, queries, out_grad, resp_keys, resp_values, prompt_rows, kept, *earlier)


def whole(kernel, out_shape, spaces, *operands, params=SMALL, **more):
    return pl.pallas_call(
        kernel,
        out_shape=out_shape,
        in_specs=[pl.BlockSpec(memory_space=space) for space in spaces],
        compiler_params=params,
        **more,
    )(*operands)


def low(*shape):
    return jax.ShapeDtypeStruct(shape, jnp.bfloat16)


def shards(
    queries, resp_keys, resp_values, out_grad, prompt_keys, prompt_values, lengths, prompt_of
):
    pieces = over_store(
        whole(
            stored_kernel,
            low(PROMPTS * LANES, SENT, HD),
            [pltpu.HBM] * 3,
            prompt_of,
            prompt_keys,
            prompt_values,
            params=FIRST,
            scratch_shapes=[
                pltpu.SMEM(prompt_of.shape, jnp.int32),
                pltpu.VMEM(prompt_keys.shape, jnp.bfloat16),
                pltpu.VMEM(prompt_values.shape, jnp.bfloat16),
                pltpu.SemaphoreType.DMA((3,)),
            ],
        )
    )
    *rows, token = stack(queries, out_grad, lengths.shape[0])
    picked, owners = whole(
        pick_kernel,
        (low(MEMBERS, LOCAL, SLICE, HD), jax.ShapeDtypeStruct((MEMBERS, HD), jnp.int32)),
        [pltpu.VMEM, pl.ANY],
        pieces,
        token,
        scratch_shapes=[pltpu.SMEM((MEMBERS, HD), jnp.int32), pltpu.SemaphoreType.DMA],
    )
    prompt_rows = over_pick(picked).reshape(2, KV_LANE, GROUPS, LOCAL, SLICE, HD)
    shared = (lengths, *rows, resp_keys, resp_values, prompt_rows)
    terms, kept = attend(*shared)
    terms = over_pick(terms.reshape(MEMBERS, LOCAL, SLICE, HD))
    *results, token = outputs(*shared, kept)
    sums = whole(
        fold_kernel,
        low(PROMPTS * LANES, TILE, HD),
        [pltpu.SMEM, pltpu.VMEM, pl.ANY],
        owners,
        terms,
        token,
        scratch_shapes=[pltpu.VMEM((PROMPTS, SLICE, HD), jnp.float32)],
    )
    *results, token = outputs(*shared, kept, HALF, (*results, sums))
    prompt_key_grad, prompt_value_grad = whole(
        summed_kernel,
        (low(*prompt_keys.shape), low(*prompt_values.shape)),
        [pltpu.VMEM, pl.ANY],
        over_store(sums),
        token,
    )
    return (*results, prompt_key_grad, prompt_value_grad)


def solution(mesh):
    wide = P("resp", "tp")
    stored = P(("resp", "tp"), None)
    return jax.shard_map(
        shards,
        mesh=mesh,
        in_specs=(wide, wide, wide, wide, stored, stored, P("resp"), P("resp")),
        out_specs=(wide, wide, wide, wide, stored, stored),
        check_vma=False,
    )
```

```python
import functools

import jax
import jax.numpy as jnp
from jax import lax
from jax.experimental import pallas as pl
from jax.experimental.pallas import tpu as pltpu
from jax.sharding import PartitionSpec as P

HD = 128
LP = 256
ROWS = 32
PER_GROUP = 8
KV_LANE = 2
LANES = 4
GROUPS = 4
TILE = 16
MEMBERS = 16
PROMPTS = 16
LOCAL = 4
SLICE = LP // GROUPS
CHUNKS = 5
HALF = LOCAL // 2
SENT = TILE + 8
LOG2E = 1.4426950408889634
LARGE = pltpu.CompilerParams(vmem_limit_bytes=48 * 1024 * 1024)
FIRST = pltpu.CompilerParams(vmem_limit_bytes=(64 * 1024 - 64) * 1024)
SMALL = pltpu.CompilerParams(vmem_limit_bytes=16 * 1024 * 1024)

STORE_GROUPS = [
    [(p * 4 + (turn + t) % 4) * 4 + t for p in range(PROMPTS) for t in range(LANES)]
    for turn in range(4)
]
PICK_GROUPS = [
    [z * 32 + x * 8 + high * 4 + block for x in range(4) for block in range(4)]
    for z in range(2)
    for high in range(2)
]


def over_store(array):
    return lax.all_to_all(
        array,
        ("resp", "tp"),
        split_axis=0,
        concat_axis=0,
        tiled=True,
        axis_index_groups=STORE_GROUPS,
    )


def over_pick(array):
    return lax.all_to_all(
        array, "resp", split_axis=0, concat_axis=0, tiled=True, axis_index_groups=PICK_GROUPS
    )


def column_of(x):
    return (x // KV_LANE, x % KV_LANE)


def stored_kernel(
    owner_hbm, key_hbm, value_hbm, out_ref, owner_ref, key_ref, value_ref, sems
):
    copies = [
        pltpu.make_async_copy(source, target, sems.at[at])
        for at, (source, target) in enumerate(
            ((owner_hbm, owner_ref), (key_hbm, key_ref), (value_hbm, value_ref))
        )
    ]
    for copy in copies:
        copy.start()
    for copy in copies:
        copy.wait()
    at = lax.broadcasted_iota(jnp.int32, (SENT - TILE, HD), 1)
    asked = jnp.zeros((SENT - TILE, HD), jnp.int32)
    for one in range(LOCAL):
        asked = jnp.where(at == one, owner_ref[one], asked)
    asked = asked.astype(jnp.float32).astype(jnp.bfloat16)
    for prompt in range(PROMPTS):
        which, head = column_of(prompt // 2 % 4)
        source = value_ref if which else key_ref
        for lane in range(LANES):
            first = (lane * KV_LANE + head) * HD
            out_ref[prompt * LANES + lane] = jnp.concatenate(
                [source[:, first : first + HD], asked], 0
            )


def pick_kernel(pieces_ref, out_ref, owner_ref, owners, sem):
    resp = lax.axis_index("resp")
    prompt = resp // 4
    turn = (resp % 4 + LANES - lax.axis_index("tp")) % 4
    for x in range(4):
        for block in range(4):
            source = (prompt // 8 * 8 + x * 2 + prompt % 2) * LANES + (block + 4 - turn) % 4
            tile = pieces_ref[source].astype(jnp.float32)
            owner_ref[x * 4 + block : x * 4 + block + 1] = tile[TILE : TILE + 1].astype(jnp.int32)
    copy = pltpu.make_async_copy(owner_ref, owners, sem)
    copy.start()
    copy.wait()
    for member in range(MEMBERS):
        for one in range(LOCAL):
            owner = owners[member, one]
            for lane in range(LANES):
                out_ref[member, one, lane * TILE : (lane + 1) * TILE] = pieces_ref[
                    owner * LANES + lane, :TILE
                ]


def fold_kernel(owner_ref, terms_ref, token_ref, out_ref, total):
    total[...] = jnp.zeros_like(total)
    for one in range(LOCAL):
        for member in range(MEMBERS):
            owner = owner_ref[member, one]
            total[owner] += terms_ref[member, one].astype(jnp.float32)
    for prompt in range(PROMPTS):
        for lane in range(LANES):
            out_ref[prompt * LANES + lane] = total[
                prompt, lane * TILE : (lane + 1) * TILE
            ].astype(out_ref.dtype)


def summed_kernel(sums_ref, token_ref, key_ref, value_ref):
    for x in range(4):
        which, head = column_of(x)
        target = value_ref if which else key_ref
        for lane in range(LANES):
            tile = jnp.zeros((TILE, HD), jnp.float32)
            for z in range(2):
                for high in range(2):
                    source = (z * 8 + x * 2 + high) * LANES + lane
                    tile = tile + sums_ref[source].astype(jnp.float32)
            first = (lane * KV_LANE + head) * HD
            target[:, first : first + HD] = tile.astype(target.dtype)


def stacked(ref, head, first):
    parts = [ref[first : first + ROWS, column] for _, column in heads(head)]
    return jnp.concatenate(parts, 0)


def heads(head):
    for at in range(PER_GROUP):
        column = (head * PER_GROUP + at) * HD
        yield slice(at * ROWS, (at + 1) * ROWS), slice(column, column + HD)


def by_length(length, span, work, blank):
    for first in range(0, span, 2 * ROWS):
        second = first + ROWS
        last = min(second + ROWS, span)
        if second < span:

            @pl.when(length > second)
            def _():
                work((first, second))

        @pl.when((length > first) & ((length <= second) | (second >= span)))
        def _():
            work((first,))
            if second < span:
                blank(second, last)

        @pl.when(length <= first)
        def _():
            blank(first, last)


def kept_copies(kept, held, sems, response, slot, head, first, out):
    chunk = first // ROWS
    rows = pl.ds(0, LP + first + ROWS)
    for at in range(2):
        far = kept.at[response, at, head, chunk, rows]
        near = held[at].at[slot, head, chunk, rows]
        source, target = (near, far) if out else (far, near)
        yield pltpu.make_async_copy(source, target, sems.at[slot, head, chunk, at])


def each_live(length_ref, start, count, span, act):
    for slot in range(count):
        for first in range(0, span, ROWS):

            @pl.when(length_ref[start + slot] > first)
            def _():
                for head in range(KV_LANE):
                    act(start + slot, slot, head, first)


def attend_kernel(
    length_ref,
    query_ref,
    grad_ref,
    key_ref,
    value_ref,
    prompt_ref,
    prompt_grad_ref,
    kept,
    keys,
    values,
    scores,
    prob_grads,
    probability_ref,
    score_grad_ref,
    key_total,
    value_total,
    sems,
):
    held = (probability_ref, score_grad_ref)
    response = pl.program_id(0)
    length = length_ref[response]
    span = key_ref.shape[0]
    scale = HD**-0.5
    wide = PER_GROUP * ROWS
    for head in range(KV_LANE):
        for whole, own_ref, which in ((keys, key_ref, 0), (values, value_ref, 1)):
            whole[head, :LP] = prompt_ref[which, head, :, 0].reshape(LP, HD)
            whole[head, LP:] = own_ref[:, head * HD : (head + 1) * HD]

    def score(slot, head, first):
        count = LP + first + ROWS
        lane = lax.broadcasted_iota(jnp.int32, (1, wide), 1) % ROWS
        causal = lax.broadcasted_iota(jnp.int32, (ROWS, 1), 0) <= lane
        raw = lax.dot_general(
            keys[head, :count],
            stacked(query_ref, head, first),
            (((1,), (1,)), ((), ())),
            preferred_element_type=jnp.float32,
        )
        tail = jnp.where(causal, raw[count - ROWS :], -1e30)
        scores[slot, : count - ROWS] = raw[: count - ROWS]
        scores[slot, count - ROWS : count] = tail
        top = jnp.max(raw[: count - ROWS].reshape(-1, 8, wide), axis=0)
        top = jnp.maximum(top, jnp.max(tail.reshape(-1, 8, wide), axis=0))
        prob_grads[slot, :count] = lax.dot_general(
            values[head, :count],
            stacked(grad_ref, head, first),
            (((1,), (1,)), ((), ())),
            preferred_element_type=jnp.float32,
        )
        return jnp.max(top, axis=0, keepdims=True) * (scale * LOG2E)

    def soften(slot, head, first, largest):
        count = LP + first + ROWS
        chunk = first // ROWS
        lane = lax.broadcasted_iota(jnp.int32, (1, wide), 1) % ROWS
        live = first + lane < length
        blocks = [slice(at, at + ROWS) for at in range(0, count, ROWS)]
        total = jnp.zeros((8, wide), jnp.float32)
        moved = jnp.zeros((8, wide), jnp.float32)
        for block in blocks:
            weights = jnp.exp2(scores[slot, block] * (scale * LOG2E) - largest)
            scores[slot, block] = weights
            total = total + jnp.sum(weights.reshape(-1, 8, wide), axis=0)
            terms = weights * prob_grads[slot, block]
            moved = moved + jnp.sum(terms.reshape(-1, 8, wide), axis=0)
        inverse = jnp.where(live, 1.0 / jnp.sum(total, axis=0, keepdims=True), 0.0)
        delta = jnp.sum(moved, axis=0, keepdims=True) * inverse
        for block in blocks:
            probability = scores[slot, block] * inverse
            probability_ref[response, head, chunk, block] = probability.astype(jnp.bfloat16)
            score_grad_ref[response, head, chunk, block] = (
                probability * (prob_grads[slot, block] - delta)
            ).astype(jnp.bfloat16)

    def gather(head, first):
        for total, left_ref, right_ref in (
            (value_total, probability_ref, grad_ref),
            (key_total, score_grad_ref, query_ref),
        ):
            terms = jnp.dot(
                left_ref[response, head, first // ROWS, :LP],
                stacked(right_ref, head, first),
                preferred_element_type=jnp.float32,
            )
            if first == 0:
                total[head] = terms
            else:
                total[head] += terms

    def work(firsts):
        streams = [(head, first) for first in firsts for head in range(KV_LANE)]
        largest = {0: score(0, *streams[0])}
        for slot, stream in enumerate(streams):
            if slot + 1 < len(streams):
                largest[slot + 1] = score(slot + 1, *streams[slot + 1])
            soften(slot, *stream, largest[slot])
            for copy in kept_copies(kept, held, sems, response, response, *stream, True):
                copy.start()
            if slot > 0:
                gather(*streams[slot - 1])
        gather(*streams[-1])

    by_length(length, span, work, lambda first, last: None)

    for head in range(KV_LANE):
        key_terms = (key_total[head] * scale).astype(jnp.bfloat16)
        value_terms = value_total[head].astype(jnp.bfloat16)
        prompt_grad_ref[0, head, :, 0] = key_terms.reshape(GROUPS, SLICE, HD)
        prompt_grad_ref[1, head, :, 0] = value_terms.reshape(GROUPS, SLICE, HD)

    def finish(*chunk):
        for copy in kept_copies(kept, held, sems, *chunk, True):
            copy.wait()

    @pl.when(response == LOCAL - 1)
    def _():
        each_live(length_ref, 0, LOCAL, span, finish)


def outputs_kernel(
    start, length_ref, query_ref, grad_ref, key_ref, value_ref, prompt_ref, kept, *rest
):
    out_ref, query_grad_ref, key_grad_ref, value_grad_ref, token_ref, *rest = rest[-12:]
    keys_t, values_t, probability_ref, score_grad_ref, key_total, value_total, sems = rest
    held = (probability_ref, score_grad_ref)
    slot = pl.program_id(0)
    response = start + slot
    length = length_ref[response]
    span = out_ref.shape[0]
    scale = HD**-0.5

    def fetch(*chunk):
        for copy in kept_copies(kept, held, sems, *chunk, False):
            copy.start()

    @pl.when(slot == 0)
    def _():
        each_live(length_ref, start, HALF, span, fetch)

    for head in range(KV_LANE):
        lanes = slice(head * HD, (head + 1) * HD)
        for whole_t, own_ref, which in ((keys_t, key_ref, 0), (values_t, value_ref, 1)):
            whole_t[head] = jnp.concatenate(
                [prompt_ref[which, head, :, 0].reshape(LP, HD), own_ref[:, lanes]], 0
            ).T

    def work(firsts):
        for first in firsts:
            count = LP + first + ROWS
            chunk = first // ROWS
            rows = slice(first, first + ROWS)
            for head in range(KV_LANE):
                for copy in kept_copies(kept, held, sems, response, slot, head, first, False):
                    copy.wait()
            for head in range(KV_LANE):
                output = jnp.dot(
                    values_t[head, :, :count],
                    probability_ref[slot, head, chunk, :count],
                    preferred_element_type=jnp.float32,
                )
                query_grad = jnp.dot(
                    keys_t[head, :, :count],
                    score_grad_ref[slot, head, chunk, :count],
                    preferred_element_type=jnp.float32,
                )
                output = output.astype(jnp.bfloat16).T
                query_grad = (query_grad * scale).astype(jnp.bfloat16).T
                for part, column in heads(head):
                    out_ref[rows, column] = output[part]
                    query_grad_ref[rows, column] = query_grad[part]
                for total, left_ref, right_ref in (
                    (value_total, probability_ref, grad_ref),
                    (key_total, score_grad_ref, query_ref),
                ):
                    terms = jnp.dot(
                        left_ref[slot, head, chunk, LP:count],
                        stacked(right_ref, head, first),
                        preferred_element_type=jnp.float32,
                    )
                    if first > 0:
                        total[head, :first] += terms[:first]
                    total[head, rows] = terms[first:]

    def blank(first, last):
        zeros = jnp.zeros((last - first, out_ref.shape[1]), jnp.bfloat16)
        out_ref[first:last, :] = zeros
        query_grad_ref[first:last, :] = zeros
        zeros = jnp.zeros((KV_LANE, last - first, HD), jnp.float32)
        key_total[:, first:last] = zeros
        value_total[:, first:last] = zeros

    by_length(length, span, work, blank)
    for head in range(KV_LANE):
        lanes = slice(head * HD, (head + 1) * HD)
        key_grad_ref[:, lanes] = (key_total[head] * scale).astype(jnp.bfloat16)
        value_grad_ref[:, lanes] = value_total[head].astype(jnp.bfloat16)
    token_ref[...] = jnp.zeros_like(token_ref)


def specs(span, wide, narrow, start=0):
    return dict(
        wide=pl.BlockSpec((span, wide), lambda i, length: (start + i, 0)),
        narrow=pl.BlockSpec((span, narrow), lambda i, length: (start + i, 0)),
        prompt=pl.BlockSpec(
            (2, KV_LANE, GROUPS, 1, SLICE, HD), lambda i, length: (0, 0, 0, start + i, 0, 0)
        ),
        kept=pl.BlockSpec(memory_space=pl.ANY),
    )


def attend(lengths, queries, out_grad, resp_keys, resp_values, prompt_rows):
    count = lengths.shape[0]
    span = queries.shape[0] // count
    both = LP + span
    streams = 2 * KV_LANE
    wide = PER_GROUP * ROWS
    spec = specs(span, queries.shape[1], resp_keys.shape[1])
    held = (count, KV_LANE, CHUNKS, both, wide)
    return pl.pallas_call(
        attend_kernel,
        out_shape=(
            jax.ShapeDtypeStruct(prompt_rows.shape, jnp.bfloat16),
            jax.ShapeDtypeStruct((count, 2, KV_LANE, CHUNKS, both, wide), jnp.bfloat16),
        ),
        grid_spec=pltpu.PrefetchScalarGridSpec(
            num_scalar_prefetch=1,
            grid=(count,),
            in_specs=[spec[name] for name in ("wide", "wide", "narrow", "narrow", "prompt")],
            out_specs=[spec[name] for name in ("prompt", "kept")],
            scratch_shapes=[
                pltpu.VMEM((KV_LANE, both, HD), jnp.bfloat16),
                pltpu.VMEM((KV_LANE, both, HD), jnp.bfloat16),
                pltpu.VMEM((streams, both, wide), jnp.float32),
                pltpu.VMEM((streams, both, wide), jnp.float32),
                pltpu.VMEM(held, jnp.bfloat16),
                pltpu.VMEM(held, jnp.bfloat16),
                pltpu.VMEM((KV_LANE, LP, HD), jnp.float32),
                pltpu.VMEM((KV_LANE, LP, HD), jnp.float32),
                pltpu.SemaphoreType.DMA((count, KV_LANE, CHUNKS, 2)),
            ],
        ),
        compiler_params=LARGE,
        cost_estimate=pl.CostEstimate(
            flops=16 * queries.size * both,
            bytes_accessed=4 * queries.size,
            transcendentals=queries.size * both // HD,
        ),
    )(lengths, queries, out_grad, resp_keys, resp_values, prompt_rows)


def outputs(
    lengths, queries, out_grad, resp_keys, resp_values, prompt_rows, kept, start=0, earlier=()
):
    rows, wide = queries.shape
    span = rows // lengths.shape[0]
    both = LP + span
    spec = specs(span, wide, resp_keys.shape[1], start)
    held = (HALF, KV_LANE, CHUNKS, both, PER_GROUP * ROWS)
    shape = jax.ShapeDtypeStruct(queries.shape, jnp.bfloat16)
    own = jax.ShapeDtypeStruct(resp_keys.shape, jnp.bfloat16)
    return pl.pallas_call(
        functools.partial(outputs_kernel, start),
        out_shape=(shape, shape, own, own, jax.ShapeDtypeStruct((8, HD), jnp.int32)),
        grid_spec=pltpu.PrefetchScalarGridSpec(
            num_scalar_prefetch=1,
            grid=(HALF,),
            in_specs=[spec[name] for name in ("wide", "wide", "narrow", "narrow", "prompt", "kept")]
            + [spec["kept"]] * len(earlier),
            out_specs=[
                spec["wide"],
                spec["wide"],
                spec["narrow"],
                spec["narrow"],
                pl.BlockSpec((8, HD), lambda i, length: (0, 0)),
            ],
            scratch_shapes=[
                pltpu.VMEM((KV_LANE, HD, both), jnp.bfloat16),
                pltpu.VMEM((KV_LANE, HD, both), jnp.bfloat16),
                pltpu.VMEM(held, jnp.bfloat16),
                pltpu.VMEM(held, jnp.bfloat16),
                pltpu.VMEM((KV_LANE, span, HD), jnp.float32),
                pltpu.VMEM((KV_LANE, span, HD), jnp.float32),
                pltpu.SemaphoreType.DMA((HALF, KV_LANE, CHUNKS, 2)),
            ],
        ),
        input_output_aliases={7 + at: at for at in range(len(earlier[:4]))},
        compiler_params=LARGE,
        cost_estimate=pl.CostEstimate(
            flops=4 * rows * wide * both,
            bytes_accessed=2 * rows * wide + kept.size,
            transcendentals=0,
        ),
    )(lengths, queries, out_grad, resp_keys, resp_values, prompt_rows, kept, *earlier)


def whole(kernel, out_shape, spaces, *operands, params=SMALL, **more):
    return pl.pallas_call(
        kernel,
        out_shape=out_shape,
        in_specs=[pl.BlockSpec(memory_space=space) for space in spaces],
        compiler_params=params,
        **more,
    )(*operands)


def low(*shape):
    return jax.ShapeDtypeStruct(shape, jnp.bfloat16)


def shards(
    queries, resp_keys, resp_values, out_grad, prompt_keys, prompt_values, lengths, prompt_of
):
    pieces = over_store(
        whole(
            stored_kernel,
            low(PROMPTS * LANES, SENT, HD),
            [pltpu.HBM] * 3,
            prompt_of,
            prompt_keys,
            prompt_values,
            params=FIRST,
            scratch_shapes=[
                pltpu.SMEM(prompt_of.shape, jnp.int32),
                pltpu.VMEM(prompt_keys.shape, jnp.bfloat16),
                pltpu.VMEM(prompt_values.shape, jnp.bfloat16),
                pltpu.SemaphoreType.DMA((3,)),
            ],
        )
    )
    picked, owners = whole(
        pick_kernel,
        (low(MEMBERS, LOCAL, SLICE, HD), jax.ShapeDtypeStruct((MEMBERS, HD), jnp.int32)),
        [pltpu.VMEM],
        pieces,
        scratch_shapes=[pltpu.SMEM((MEMBERS, HD), jnp.int32), pltpu.SemaphoreType.DMA],
    )
    prompt_rows = over_pick(picked).reshape(2, KV_LANE, GROUPS, LOCAL, SLICE, HD)
    shared = (lengths, queries, out_grad, resp_keys, resp_values, prompt_rows)
    terms, kept = attend(*shared)
    terms = over_pick(terms.reshape(MEMBERS, LOCAL, SLICE, HD))
    *results, token = outputs(*shared, kept)
    sums = whole(
        fold_kernel,
        low(PROMPTS * LANES, TILE, HD),
        [pltpu.SMEM, pltpu.VMEM, pl.ANY],
        owners,
        terms,
        token,
        scratch_shapes=[pltpu.VMEM((PROMPTS, SLICE, HD), jnp.float32)],
    )
    *results, token = outputs(*shared, kept, HALF, (*results, sums))
    prompt_key_grad, prompt_value_grad = whole(
        summed_kernel,
        (low(*prompt_keys.shape), low(*prompt_values.shape)),
        [pltpu.VMEM, pl.ANY],
        over_store(sums),
        token,
    )
    return (*results, prompt_key_grad, prompt_value_grad)


def solution(mesh):
    wide = P("resp", "tp")
    stored = P(("resp", "tp"), None)
    return jax.shard_map(
        shards,
        mesh=mesh,
        in_specs=(wide, wide, wide, wide, stored, stored, P("resp"), P("resp")),
        out_specs=(wide, wide, wide, wide, stored, stored),
        check_vma=False,
    )
```
